32 devices in a mesh: pipe: 4 (over y, core), dp: 4 (over z), tensor: 2 (over x).
Axes of the slice: x: 2, y: 2, z: 4, core: 2. Of those that a mesh axis runs over, the one named last changes fastest.
Arguments:
- grad_out: bfloat16 [4, 4, 4, 96, 6144], P('pipe', None, 'dp'), may hold values from -6 to 6
- qkv_saved: bfloat16 [4, 4, 4, 96, 2, 384], P('pipe', None, 'dp', None, 'tensor'), may hold values from -5 to 5
- w_out: bfloat16 [4, 6144, 2, 128], P('pipe', None, 'tensor'), may hold values from -0.078125 to 0.078125
- w_qkv: bfloat16 [4, 6144, 2, 384], P('pipe', None, 'tensor'), may hold values from -0.21875 to 0.21875
- plan: int32 [4, 4], P('pipe'), may hold values from 0 to 3, each once within a row
Outputs:
- input_grad: bfloat16 [4, 4, 96, 2, 6144], P('pipe', 'dp', 'tensor')
- out_proj_grad: float32 [4, 6144, 2, 128], P('pipe', 'dp', 'tensor')
The draws below stay inside these ranges and needn't reach their ends.
All inputs are finite; a program needn't handle non-finite values.
Results may differ from the reference program's by a relative error of at most 0.028.
Values may be sent and summed in bfloat16 or wider, within the bound.
A program may use at most 64 MiB of HBM per device.

```python
from functools import reduce
import jax
import jax.numpy as jnp
from jax import lax

D = 6144
HEAD = 128
SEQ = 96
MICRO = 4
BMICRO = 2
SECTIONS = 4
SEQS = 4
HEADS = 2


def draw_qkv_saved(key, part):
    shape = (SECTIONS, MICRO, SEQS, SEQ, HEADS, 3 * HEAD)
    first_key = jax.random.fold_in(key, 11)
    entries = jnp.clip(jax.random.normal(first_key, shape, jnp.float32), -4.0, 4.0)
    return entries.astype(jnp.bfloat16)


def strengthened(result, rng, source, target, parts, factor):
    def block_of(dim):
        return (jnp.arange(result.shape[dim]) // (result.shape[dim] // parts)).reshape((-1,) + (1,) * (result.ndim - 1 - dim))

    first = jax.random.permutation(rng, parts)[block_of(target)]
    far = (block_of(target) + parts // 2) % parts
    return jnp.where((block_of(source) == first) | (block_of(source) == far), factor * result, result)


def block_scale(key, shape, shards, low, largest):
    def one(dim, parts):
        heights = jax.random.uniform(jax.random.fold_in(jax.random.fold_in(key, 6), dim), (parts,), jnp.float32, low / len(shards), largest / len(shards))
        return jnp.repeat(jnp.exp(heights), shape[dim] // parts).reshape((-1,) + (1,) * (len(shape) - dim - 1))

    level = one(*shards[0])
    for cut in shards[1:]:
        level = level * one(*cut)
    return level


def normal_values(own_key, extent, width, bound, pieces=(), held_as=jnp.bfloat16):
    values = width * jax.random.normal(own_key, extent, jnp.float32)
    if pieces:
        values = values * block_scale(own_key, extent, pieces, -0.22, 0.18)
    return jnp.clip(values, -bound, bound).astype(held_as)


def heavy_noise(key, extent, deviation, limit, split, heavy, kind=jnp.bfloat16):
    values = deviation * jax.random.normal(key, extent, jnp.float32)
    if split:
        values = values * block_scale(key, extent, split, -0.22, 0.18)
    return jnp.clip(strengthened(values, jax.random.fold_in(key, 3), *heavy), -limit, limit).astype(kind)


def setup_inputs(seed: int = 0) -> dict:
    arg_keys = jax.random.split(jax.random.key(seed), 6)
    grad_out = heavy_noise(arg_keys[0], (SECTIONS, MICRO, SEQS, SEQ, D), 1.0, 6.0, ((0, 4), (2, 4)), (2, 4, 4, 2.0))
    qkv_saved = draw_qkv_saved(jax.random.fold_in(arg_keys[5], 71), 0)
    w_out = normal_values(arg_keys[2], (SECTIONS, D, HEADS, HEAD), D ** -0.5, 0.078125, ((0, 4), (2, 2)))
    w_qkv = normal_values(arg_keys[3], (SECTIONS, D, HEADS, 3 * HEAD), (3 * HEAD * HEADS) ** -0.5, 0.21875, ((0, 4), (2, 2)))
    plan = jax.vmap(lambda own: jax.random.permutation(own, MICRO))(jax.random.split(arg_keys[4], SECTIONS)).reshape((SECTIONS, MICRO)).astype(jnp.int32)
    return {"grad_out": grad_out, "qkv_saved": qkv_saved, "w_out": w_out, "w_qkv": w_qkv, "plan": plan}


def head_forward(queries, key_rows, values):
    score_scale = HEAD ** -0.5
    scores = jnp.dot(queries, key_rows.T, preferred_element_type=jnp.float32) * score_scale
    row_ids = lax.broadcasted_iota(jnp.int32, scores.shape, 0)
    col_ids = lax.broadcasted_iota(jnp.int32, scores.shape, 1)
    scores = jnp.where(col_ids <= row_ids, scores, -1e30)
    row_max = jnp.max(scores, axis=1, keepdims=True)
    weights = jnp.exp(scores - row_max)
    softmax = weights / jnp.sum(weights, axis=1, keepdims=True)
    soft_low = softmax.astype(jnp.bfloat16)
    attended = jnp.dot(soft_low, values, preferred_element_type=jnp.float32).astype(jnp.bfloat16)
    return softmax, soft_low, attended


def head_backward(queries, key_rows, values, grad_head):
    score_scale = HEAD ** -0.5
    softmax, soft_low, attended = head_forward(queries, key_rows, values)
    row_dot = jnp.sum(grad_head.astype(jnp.float32) * attended.astype(jnp.float32), axis=1, keepdims=True)
    grad_values = jnp.dot(soft_low.T, grad_head, preferred_element_type=jnp.float32)
    grad_probs = jnp.dot(grad_head, values.T, preferred_element_type=jnp.float32)
    grad_scores = (softmax * (grad_probs - row_dot)).astype(jnp.bfloat16)
    grad_query = jnp.dot(grad_scores, key_rows, preferred_element_type=jnp.float32) * score_scale
    grad_keys = jnp.dot(grad_scores.T, queries, preferred_element_type=jnp.float32) * score_scale
    return jnp.concatenate([grad_query, grad_keys, grad_values], axis=1).astype(jnp.bfloat16)


def one_sequence(grad_seq, qkv_seq, out_proj, qkv_proj, order):
    input_parts = []
    weight_parts = []
    for head_index in range(HEADS):
        block = qkv_seq[:, :, head_index, :]
        weight_head = jnp.zeros((D, HEAD), jnp.float32)
        for micro_index in range(MICRO):
            chosen = block[micro_index]
            softmax, soft_low, attended = head_forward(chosen[:, :HEAD], chosen[:, HEAD:2 * HEAD], chosen[:, 2 * HEAD:])
            weight_head = weight_head + jnp.dot(grad_seq[micro_index].T, attended, preferred_element_type=jnp.float32)
        weight_parts.append(weight_head)
        head_terms = []
        for slot_index in range(BMICRO):
            picked = order[slot_index]
            chosen = block[picked]
            grad_rows = grad_seq[picked]
            grad_head = jnp.dot(grad_rows, out_proj[:, head_index, :], preferred_element_type=jnp.float32).astype(jnp.bfloat16)
            grad_qkv = head_backward(chosen[:, :HEAD], chosen[:, HEAD:2 * HEAD], chosen[:, 2 * HEAD:], grad_head)
            term = jnp.dot(grad_qkv, qkv_proj[:, head_index, :].T, preferred_element_type=jnp.float32).astype(jnp.bfloat16)
            term = lax.optimization_barrier(term).astype(jnp.float32)
            head_terms.append(term)
        input_parts.append(jnp.stack(head_terms, axis=1))
    summed = reduce(lambda left, right: left + right, input_parts)
    return summed.astype(jnp.bfloat16), jnp.stack(weight_parts, axis=1)


def reference(grad_out, qkv_saved, w_out, w_qkv, plan):
    def one_section(section_args):
        grad_section, qkv_section, out_proj, qkv_proj, order = section_args

        def advance(carry, seq_args):
            grad_seq, qkv_seq = seq_args
            input_seq, weight_seq = one_sequence(grad_seq, qkv_seq, out_proj, qkv_proj, order)
            return carry + weight_seq, input_seq

        start = jnp.zeros((D, HEADS, HEAD), jnp.float32)
        weight_total, inputs = lax.scan(advance, start, (jnp.moveaxis(grad_section, 1, 0), jnp.moveaxis(qkv_section, 1, 0)))
        return inputs, weight_total

    inputs, weights = lax.map(one_section, (grad_out, qkv_saved, w_out, w_qkv, plan))
    shifted = jnp.concatenate([inputs[1:], jnp.zeros_like(inputs[:1])], axis=0)
    return shifted, weights
```

```python
import functools

import jax
import jax.numpy as jnp
from jax import lax
from jax.experimental import pallas as pl
from jax.experimental.pallas import tpu as pltpu
from jax.sharding import PartitionSpec as P

BMICRO = 2
PIECES = 8
PARTS = 2
MESH = pl.DeviceIdType.MESH


def shifted(block, axis, distance):
    devices = range(lax.axis_size(axis))
    route = [(i - distance, i) for i in devices if i - distance in devices]
    return lax.ppermute(block, axis, route)


def head_forward(queries, key_rows, values):
    score_scale = queries.shape[-1] ** (-0.5)
    scores = jnp.dot(queries, key_rows.T, preferred_element_type=jnp.float32) * score_scale
    row_ids = lax.broadcasted_iota(jnp.int32, scores.shape, 0)
    col_ids = lax.broadcasted_iota(jnp.int32, scores.shape, 1)
    scores = jnp.where(col_ids <= row_ids, scores, -1e30)
    row_max = jnp.max(scores, axis=1, keepdims=True)
    weights = jnp.exp(scores - row_max)
    softmax = weights / jnp.sum(weights, axis=1, keepdims=True)
    soft_low = softmax.astype(jnp.bfloat16)
    attended = jnp.dot(soft_low, values, preferred_element_type=jnp.float32).astype(jnp.bfloat16)
    return (softmax, soft_low, attended)


def head_backward(queries, key_rows, values, softmax, soft_low, attended, grad_head):
    score_scale = queries.shape[-1] ** (-0.5)
    row_dot = jnp.sum(
        grad_head.astype(jnp.float32) * attended.astype(jnp.float32), axis=1, keepdims=True
    )
    grad_values = jnp.dot(soft_low.T, grad_head, preferred_element_type=jnp.float32)
    grad_probs = jnp.dot(grad_head, values.T, preferred_element_type=jnp.float32)
    grad_scores = (softmax * (grad_probs - row_dot)).astype(jnp.bfloat16)
    grad_query = jnp.dot(grad_scores, key_rows, preferred_element_type=jnp.float32) * score_scale
    grad_keys = jnp.dot(grad_scores.T, queries, preferred_element_type=jnp.float32) * score_scale
    return jnp.concatenate([grad_query, grad_keys, grad_values], axis=1).astype(jnp.bfloat16)


def body(grad_out, qkv_saved, w_out, w_qkv, plan):
    gradients = grad_out[0, :, 0]
    saved_qkv = qkv_saved[0, :, 0, :, 0]
    out_proj = w_out[0, :, 0]
    qkv_proj = w_qkv[0, :, 0]
    head_size = out_proj.shape[1]
    seq_len = gradients.shape[1]
    queries = saved_qkv[:, :, :head_size]
    key_rows = saved_qkv[:, :, head_size : 2 * head_size]
    values = saved_qkv[:, :, 2 * head_size :]
    softmax, soft_low, attended = jax.vmap(head_forward)(queries, key_rows, values)
    current = plan[0, :BMICRO]
    grad_current = jnp.take(gradients, current, axis=0)
    grad_heads = jnp.einsum(
        "msd,dh->msh", grad_current, out_proj, preferred_element_type=jnp.float32
    ).astype(jnp.bfloat16)
    grad_qkv = jax.vmap(head_backward)(
        jnp.take(queries, current, axis=0),
        jnp.take(key_rows, current, axis=0),
        jnp.take(values, current, axis=0),
        jnp.take(softmax, current, axis=0),
        jnp.take(soft_low, current, axis=0),
        jnp.take(attended, current, axis=0),
        grad_heads,
    )
    share_rows = seq_len // lax.axis_size("tensor")
    partials = jnp.einsum("bsk,dk->sbd", grad_qkv, qkv_proj, preferred_element_type=jnp.float32)
    summed = lax.psum(partials.astype(jnp.bfloat16), "tensor").astype(jnp.float32)
    own_rows = lax.dynamic_slice_in_dim(
        summed, lax.axis_index("tensor") * share_rows, share_rows, 0
    )
    received = shifted(own_rows.astype(jnp.bfloat16), "pipe", -1)
    weight_grad = lax.psum_scatter(
        jnp.einsum("msc,msh->ch", gradients, attended, preferred_element_type=jnp.float32),
        "dp",
        scatter_dimension=0,
        tiled=True,
    )
    return (received[None, None], weight_grad[None, :, None, :])


def mm(left, right, left_dim, right_dim):
    return lax.dot_general(
        left, right, (((left_dim,), (right_dim,)), ((), ())), preferred_element_type=jnp.float32
    )


def fused_kernel(
    sizes, plan_ref, g_hbm, qkv_hbm, wo_hbm, wq_hbm, in_ref, wg_ref,
    g, qkv, wo, wq, probs, att, gqkv, total, xs, own, xr, ys, rs, rr, ls, lr,
    load_sem, x_send, x_recv, y_send, y_recv, r_send, r_recv, l_send, l_recv,
):
    n, sections, micro, seq, head, features = sizes
    p = lax.axis_index("pipe")
    z = lax.axis_index("dp")
    x = lax.axis_index("tensor")
    scale = head ** (-0.5)
    half = seq // 2
    rows = BMICRO * half
    width = features // PIECES
    chunk = features // n
    part = chunk // PARTS
    items = (n - 1) * PARTS

    loads = [
        pltpu.make_async_copy(src, dst, load_sem.at[i])
        for i, (src, dst) in enumerate(((qkv_hbm, qkv), (g_hbm, g), (wo_hbm, wo), (wq_hbm, wq)))
    ]
    for load in loads:
        load.start()

    barrier = pltpu.get_barrier_semaphore()

    def greet(target):
        pl.semaphore_signal(barrier, inc=1, device_id=target, device_id_type=MESH)

    @pl.when(z > 0)
    def _():
        greet({"dp": z - 1})

    @pl.when(z < n - 1)
    def _():
        greet({"dp": z + 1})

    @pl.when(p > 0)
    def _():
        greet({"tensor": 1 - x})

    @pl.when(p < sections - 1)
    def _():
        greet({"pipe": p + 1})

    def x_copy(k):
        return pltpu.make_async_remote_copy(
            src_ref=xs.at[k], dst_ref=xr.at[k], send_sem=x_send.at[k], recv_sem=x_recv.at[k],
            device_id={"tensor": 1 - x}, device_id_type=MESH,
        )

    def y_copy(k):
        return pltpu.make_async_remote_copy(
            src_ref=ys.at[k], dst_ref=in_ref.at[:, pl.ds(k * width, width)],
            send_sem=y_send.at[k], recv_sem=y_recv.at[k],
            device_id={"pipe": p - 1}, device_id_type=MESH,
        )

    def r_copy(i):
        return pltpu.make_async_remote_copy(
            src_ref=rs.at[i], dst_ref=rr.at[i], send_sem=r_send.at[i], recv_sem=r_recv.at[i],
            device_id={"dp": z + 1}, device_id_type=MESH,
        )

    def l_copy(i):
        return pltpu.make_async_remote_copy(
            src_ref=ls.at[i], dst_ref=lr.at[i], send_sem=l_send.at[i], recv_sem=l_recv.at[i],
            device_id={"dp": z - 1}, device_id_type=MESH,
        )

    def r_columns(i):
        return pl.ds((n - 1 - i // PARTS) * chunk + (i % PARTS) * part, part)

    def l_columns(i):
        return pl.ds((i // PARTS) * chunk + (i % PARTS) * part, part)

    loads[0].wait()
    keep = lax.broadcasted_iota(jnp.int32, (seq, seq), 1) <= lax.broadcasted_iota(jnp.int32, (seq, seq), 0)
    for m in range(micro):
        scores = mm(qkv[m, :, :head], qkv[m, :, head : 2 * head], 1, 1) * scale
        scores = jnp.where(keep, scores, -1e30)
        weights = jnp.exp(scores - jnp.max(scores, axis=1, keepdims=True))
        softmax = weights / jnp.sum(weights, axis=1, keepdims=True)
        probs[m] = softmax
        att[m] = mm(softmax.astype(jnp.bfloat16), qkv[m, :, 2 * head :], 1, 0).astype(jnp.bfloat16)

    peers = lax.div(z + n - 1, n) + lax.div(2 * n - 2 - z, n) + 2 * lax.div(p + sections - 1, sections)
    pl.semaphore_wait(barrier, peers)

    loads[1].wait()

    def product(columns):
        total[:, columns] = mm(
            att[...].reshape(micro * seq, head), g[:, :, columns].reshape(micro * seq, part), 0, 0
        )

    @pl.when(z < n // 2)
    def _():
        for i in range(items + PARTS):
            columns = r_columns(i)
            product(columns)
            if i < items:

                @pl.when(z == 0)
                def _():
                    rs[i] = total[:, columns].astype(jnp.bfloat16)
                    r_copy(i).start()

    @pl.when(z >= n // 2)
    def _():
        for i in range(items + PARTS):
            columns = l_columns(i)
            product(columns)
            if i < items:

                @pl.when(z == n - 1)
                def _():
                    ls[i] = total[:, columns].astype(jnp.bfloat16)
                    l_copy(i).start()

    loads[2].wait()
    loads[3].wait()

    @pl.when(p > 0)
    def _():
        chosen = [plan_ref[0, j] for j in range(BMICRO)]
        acc = jnp.zeros((BMICRO * seq, head), jnp.float32)
        for k in range(PIECES):
            columns = pl.ds(k * width, width)
            lhs = jnp.concatenate([g[m, :, columns] for m in chosen], axis=0)
            acc = acc + mm(lhs, wo[columns, :], 1, 0)
        for j in range(BMICRO):
            m = chosen[j]
            grad_head = acc[j * seq : (j + 1) * seq].astype(jnp.bfloat16)
            softmax = probs[m]
            soft_low = softmax.astype(jnp.bfloat16)
            queries = qkv[m, :, :head]
            keys = qkv[m, :, head : 2 * head]
            values = qkv[m, :, 2 * head :]
            attended = att[m]
            row_dot = jnp.sum(
                grad_head.astype(jnp.float32) * attended.astype(jnp.float32), axis=1, keepdims=True
            )
            grad_values = mm(soft_low, grad_head, 0, 0)
            grad_probs = mm(grad_head, values, 1, 1)
            grad_scores = (softmax * (grad_probs - row_dot)).astype(jnp.bfloat16)
            gqkv[j, :, :head] = (mm(grad_scores, keys, 1, 0) * scale).astype(jnp.bfloat16)
            gqkv[j, :, head : 2 * head] = (mm(grad_scores, queries, 0, 0) * scale).astype(jnp.bfloat16)
            gqkv[j, :, 2 * head :] = grad_values.astype(jnp.bfloat16)
        theirs = pl.ds(pl.multiple_of((1 - x) * half, half), half)
        mine = pl.ds(pl.multiple_of(x * half, half), half)
        lhs = jnp.concatenate(
            [gqkv[j, theirs, :] for j in range(BMICRO)] + [gqkv[j, mine, :] for j in range(BMICRO)], axis=0
        )
        for k in range(PIECES):
            term = mm(lhs, wq[pl.ds(k * width, width), :], 1, 1).astype(jnp.bfloat16)
            xs[k] = term[:rows]
            x_copy(k).start()
            own[k] = term[rows:]

    @pl.when(p == sections - 1)
    def _():
        in_ref[...] = jnp.zeros_like(in_ref)

    def do_x(k):
        @pl.when(p > 0)
        def _():
            x_copy(k).wait_recv()
            ys[k] = (own[k].astype(jnp.float32) + xr[k].astype(jnp.float32)).astype(jnp.bfloat16)
            y_copy(k).start()

    def do_z(i):
        right_chunk = n - 1 - i // PARTS
        left_chunk = i // PARTS
        right_cols, left_cols = r_columns(i), l_columns(i)

        @pl.when((z > 0) & (z < right_chunk))
        def _():
            r_copy(i).wait_recv()
            rs[i] = (total[:, right_cols] + rr[i].astype(jnp.float32)).astype(jnp.bfloat16)
            r_copy(i).start()

        @pl.when((z < n - 1) & (z > left_chunk))
        def _():
            l_copy(i).wait_recv()
            ls[i] = (total[:, left_cols] + lr[i].astype(jnp.float32)).astype(jnp.bfloat16)
            l_copy(i).start()

        @pl.when(z == right_chunk)
        def _():
            r_copy(i).wait_recv()
            total[:, right_cols] = total[:, right_cols] + rr[i].astype(jnp.float32)

        @pl.when(z == left_chunk)
        def _():
            l_copy(i).wait_recv()
            total[:, left_cols] = total[:, left_cols] + lr[i].astype(jnp.float32)

    events = [(3.5 + 24.0 * (i + 1) / items, do_z, i) for i in range(items)]
    events += [(8.0 + 24.0 * (k + 1) / PIECES, do_x, k) for k in range(PIECES)]
    for _, act, index in sorted(events, key=lambda e: e[0]):
        act(index)

    for i in range(PARTS):
        columns = pl.ds(pl.multiple_of(z * chunk + i * part, part), part)
        wg_ref[i * part : (i + 1) * part, :] = total[:, columns].T

    @pl.when(p < sections - 1)
    def _():
        for k in range(PIECES):
            y_copy(k).wait_recv()

    @pl.when(p > 0)
    def _():
        for k in range(PIECES):
            x_copy(k).wait_send()
            y_copy(k).wait_send()

    for i in range(items):

        @pl.when(z < n - 1 - i // PARTS)
        def _():
            r_copy(i).wait_send()

        @pl.when(z > i // PARTS)
        def _():
            l_copy(i).wait_send()


def fused_body(n, sections, grad_out, qkv_saved, w_out, w_qkv, plan):
    _, micro, _, seq, features = grad_out.shape
    head = w_out.shape[-1]
    half = seq // 2
    rows = BMICRO * half
    width = features // PIECES
    part = features // n // PARTS
    items = (n - 1) * PARTS
    low, full = jnp.bfloat16, jnp.float32
    dma = pltpu.SemaphoreType.DMA
    strip = (items, head, part)
    term = (PIECES, rows, width)
    anywhere = pl.BlockSpec(memory_space=pl.ANY)
    vmem = pl.BlockSpec(memory_space=pltpu.VMEM)
    received, weight_grad = pl.pallas_call(
        functools.partial(fused_kernel, (n, sections, micro, seq, head, features)),
        out_shape=(
            jax.ShapeDtypeStruct((rows, features), low),
            jax.ShapeDtypeStruct((features // n, head), full),
        ),
        in_specs=[pl.BlockSpec(memory_space=pltpu.SMEM)] + [anywhere] * 4,
        out_specs=(vmem, vmem),
        scratch_shapes=[
            pltpu.VMEM((micro, seq, features), low),
            pltpu.VMEM((micro, seq, 3 * head), low),
            pltpu.VMEM((features, head), low),
            pltpu.VMEM((features, 3 * head), low),
            pltpu.VMEM((micro, seq, seq), full),
            pltpu.VMEM((micro, seq, head), low),
            pltpu.VMEM((BMICRO, seq, 3 * head), low),
            pltpu.VMEM((head, features), full),
        ]
        + [pltpu.VMEM(term, low)] * 4
        + [pltpu.VMEM(strip, low)] * 4
        + [dma((4,))]
        + [dma((PIECES,))] * 4
        + [dma((items,))] * 4,
        compiler_params=pltpu.CompilerParams(
            collective_id=0, has_side_effects=True, vmem_limit_bytes=56 * 1024 * 1024
        ),
        cost_estimate=pl.CostEstimate(flops=2_000_000_000, bytes_accessed=14_000_000, transcendentals=40_000),
    )(
        plan,
        grad_out.reshape(micro, seq, features),
        qkv_saved.reshape(micro, seq, 3 * head),
        w_out.reshape(features, head),
        w_qkv.reshape(features, 3 * head),
    )
    received = jnp.swapaxes(received.reshape(BMICRO, half, features), 0, 1)
    return (received[None, None], weight_grad[None, :, None, :])


def solution(mesh):
    in_specs = (
        P("pipe", None, "dp", None, None),
        P("pipe", None, "dp", None, "tensor", None),
        P("pipe", None, "tensor", None),
        P("pipe", None, "tensor", None),
        P("pipe", None),
    )
    out_specs = (P("pipe", "dp", "tensor", None, None), P("pipe", "dp", "tensor", None))
    chosen = body
    if mesh.shape["tensor"] == 2 and mesh.shape["dp"] % 2 == 0 and mesh.shape["dp"] <= 8:
        chosen = functools.partial(fused_body, mesh.shape["dp"], mesh.shape["pipe"])
    return jax.shard_map(chosen, mesh=mesh, in_specs=in_specs, out_specs=out_specs, check_vma=False)
```

```python
import functools

import jax
import jax.numpy as jnp
from jax import lax
from jax.experimental import pallas as pl
from jax.experimental.pallas import tpu as pltpu
from jax.sharding import PartitionSpec as P

BMICRO = 2
PIECES = 8
FAR = [0, 2, 4, 6]
NEAR = [1, 3, 5, 7]
PARTS = 2
MESH = pl.DeviceIdType.MESH


def shifted(block, axis, distance):
    devices = range(lax.axis_size(axis))
    route = [(i - distance, i) for i in devices if i - distance in devices]
    return lax.ppermute(block, axis, route)


def head_forward(queries, key_rows, values):
    score_scale = queries.shape[-1] ** (-0.5)
    scores = jnp.dot(queries, key_rows.T, preferred_element_type=jnp.float32) * score_scale
    row_ids = lax.broadcasted_iota(jnp.int32, scores.shape, 0)
    col_ids = lax.broadcasted_iota(jnp.int32, scores.shape, 1)
    scores = jnp.where(col_ids <= row_ids, scores, -1e30)
    row_max = jnp.max(scores, axis=1, keepdims=True)
    weights = jnp.exp(scores - row_max)
    softmax = weights / jnp.sum(weights, axis=1, keepdims=True)
    soft_low = softmax.astype(jnp.bfloat16)
    attended = jnp.dot(soft_low, values, preferred_element_type=jnp.float32).astype(jnp.bfloat16)
    return (softmax, soft_low, attended)


def head_backward(queries, key_rows, values, softmax, soft_low, attended, grad_head):
    score_scale = queries.shape[-1] ** (-0.5)
    row_dot = jnp.sum(
        grad_head.astype(jnp.float32) * attended.astype(jnp.float32), axis=1, keepdims=True
    )
    grad_values = jnp.dot(soft_low.T, grad_head, preferred_element_type=jnp.float32)
    grad_probs = jnp.dot(grad_head, values.T, preferred_element_type=jnp.float32)
    grad_scores = (softmax * (grad_probs - row_dot)).astype(jnp.bfloat16)
    grad_query = jnp.dot(grad_scores, key_rows, preferred_element_type=jnp.float32) * score_scale
    grad_keys = jnp.dot(grad_scores.T, queries, preferred_element_type=jnp.float32) * score_scale
    return jnp.concatenate([grad_query, grad_keys, grad_values], axis=1).astype(jnp.bfloat16)


def body(grad_out, qkv_saved, w_out, w_qkv, plan):
    gradients = grad_out[0, :, 0]
    saved_qkv = qkv_saved[0, :, 0, :, 0]
    out_proj = w_out[0, :, 0]
    qkv_proj = w_qkv[0, :, 0]
    head_size = out_proj.shape[1]
    seq_len = gradients.shape[1]
    queries = saved_qkv[:, :, :head_size]
    key_rows = saved_qkv[:, :, head_size : 2 * head_size]
    values = saved_qkv[:, :, 2 * head_size :]
    softmax, soft_low, attended = jax.vmap(head_forward)(queries, key_rows, values)
    current = plan[0, :BMICRO]
    grad_current = jnp.take(gradients, current, axis=0)
    grad_heads = jnp.einsum(
        "msd,dh->msh", grad_current, out_proj, preferred_element_type=jnp.float32
    ).astype(jnp.bfloat16)
    grad_qkv = jax.vmap(head_backward)(
        jnp.take(queries, current, axis=0),
        jnp.take(key_rows, current, axis=0),
        jnp.take(values, current, axis=0),
        jnp.take(softmax, current, axis=0),
        jnp.take(soft_low, current, axis=0),
        jnp.take(attended, current, axis=0),
        grad_heads,
    )
    share_rows = seq_len // lax.axis_size("tensor")
    partials = jnp.einsum("bsk,dk->sbd", grad_qkv, qkv_proj, preferred_element_type=jnp.float32)
    summed = lax.psum(partials.astype(jnp.bfloat16), "tensor").astype(jnp.float32)
    own_rows = lax.dynamic_slice_in_dim(
        summed, lax.axis_index("tensor") * share_rows, share_rows, 0
    )
    received = shifted(own_rows.astype(jnp.bfloat16), "pipe", -1)
    weight_grad = lax.psum_scatter(
        jnp.einsum("msc,msh->ch", gradients, attended, preferred_element_type=jnp.float32),
        "dp",
        scatter_dimension=0,
        tiled=True,
    )
    return (received[None, None], weight_grad[None, :, None, :])


def mm(left, right, left_dim, right_dim):
    return lax.dot_general(
        left, right, (((left_dim,), (right_dim,)), ((), ())), preferred_element_type=jnp.float32
    )


def fused_kernel(
    sizes, plan_ref, g_hbm, qkv_hbm, wo_hbm, wq_hbm, in_ref, wg_ref,
    g, qkv, wo, wq, probs, att, gqkv, total, xs, own, xr, fr, hr, fo, ys, rs, rr, ls, lr,
    load_sem, x_send, x_recv, y_send, y_recv, f_send, f_recv, h_send, h_recv, o_send, o_recv, r_send, r_recv, l_send, l_recv,
):
    n, sections, micro, seq, head, features = sizes
    p = lax.axis_index("pipe")
    z = lax.axis_index("dp")
    x = lax.axis_index("tensor")
    scale = head ** (-0.5)
    half = seq // 2
    rows = BMICRO * half
    width = features // PIECES
    chunk = features // n
    part = chunk // PARTS
    items = (n - 1) * PARTS

    loads = [
        pltpu.make_async_copy(src, dst, load_sem.at[i])
        for i, (src, dst) in enumerate(((qkv_hbm, qkv), (g_hbm, g), (wo_hbm, wo), (wq_hbm, wq)))
    ]
    loads[0].start()
    loads[1].start()

    barrier = pltpu.get_barrier_semaphore()

    def greet(target):
        pl.semaphore_signal(barrier, inc=1, device_id=target, device_id_type=MESH)

    @pl.when(z > 0)
    def _():
        greet({"dp": z - 1})

    @pl.when(z < n - 1)
    def _():
        greet({"dp": z + 1})

    @pl.when(p > 0)
    def _():
        greet({"tensor": 1 - x})

    @pl.when(p < sections - 1)
    def _():
        greet({"pipe": p + 1})

    def x_copy(k):
        return pltpu.make_async_remote_copy(
            src_ref=xs.at[k], dst_ref=xr.at[k], send_sem=x_send.at[k], recv_sem=x_recv.at[k],
            device_id={"tensor": 1 - x}, device_id_type=MESH,
        )

    def y_copy(k):
        return pltpu.make_async_remote_copy(
            src_ref=ys.at[k], dst_ref=in_ref.at[:, :, pl.ds(k * width, width)],
            send_sem=y_send.at[k], recv_sem=y_recv.at[k],
            device_id={"pipe": p - 1}, device_id_type=MESH,
        )

    def f_copy(k):
        return pltpu.make_async_remote_copy(
            src_ref=xs.at[k], dst_ref=fr.at[k // 2], send_sem=f_send.at[k // 2], recv_sem=f_recv.at[k // 2],
            device_id={"pipe": p - 1}, device_id_type=MESH,
        )

    def h_copy(k):
        return pltpu.make_async_remote_copy(
            src_ref=own.at[k], dst_ref=hr.at[k // 2], send_sem=h_send.at[k // 2], recv_sem=h_recv.at[k // 2],
            device_id={"pipe": p - 1}, device_id_type=MESH,
        )

    def o_copy(k):
        return pltpu.make_async_remote_copy(
            src_ref=fr.at[k // 2], dst_ref=fo.at[k // 2], send_sem=o_send.at[k // 2], recv_sem=o_recv.at[k // 2],
            device_id={"tensor": 1 - x}, device_id_type=MESH,
        )

    def r_copy(i):
        return pltpu.make_async_remote_copy(
            src_ref=rs.at[i], dst_ref=rr.at[i], send_sem=r_send.at[i], recv_sem=r_recv.at[i],
            device_id={"dp": z + 1}, device_id_type=MESH,
        )

    def l_copy(i):
        return pltpu.make_async_remote_copy(
            src_ref=ls.at[i], dst_ref=lr.at[i], send_sem=l_send.at[i], recv_sem=l_recv.at[i],
            device_id={"dp": z - 1}, device_id_type=MESH,
        )

    def r_columns(i):
        return pl.ds((n - 1 - i // PARTS) * chunk + (i % PARTS) * part, part)

    def l_columns(i):
        return pl.ds((i // PARTS) * chunk + (i % PARTS) * part, part)

    loads[0].wait()
    keep = lax.broadcasted_iota(jnp.int32, (seq, seq), 1) <= lax.broadcasted_iota(jnp.int32, (seq, seq), 0)
    softs = []
    for m in range(micro):
        scores = mm(qkv[m, :, :head], qkv[m, :, head : 2 * head], 1, 1) * scale
        scores = jnp.where(keep, scores, -1e30)
        weights = jnp.exp(scores - jnp.max(scores, axis=1, keepdims=True))
        softs.append(weights / jnp.sum(weights, axis=1, keepdims=True))
    outs = [
        mm(softs[m].astype(jnp.bfloat16), qkv[m, :, 2 * head :], 1, 0).astype(jnp.bfloat16)
        for m in range(micro)
    ]
    for m in range(micro):
        probs[m] = softs[m]
        att[m] = outs[m]
    loads[2].start()
    loads[3].start()

    peers = lax.div(z + n - 1, n) + lax.div(2 * n - 2 - z, n) + 2 * lax.div(p + sections - 1, sections)
    pl.semaphore_wait(barrier, peers)

    loads[1].wait()

    upper = lax.div(z, n // 2)

    def product(i):
        place = upper * (i // PARTS) + (1 - upper) * (n - 1 - i // PARTS)
        columns = pl.ds(pl.multiple_of(place * chunk + (i % PARTS) * part, part), part)
        value = mm(
            att[...].reshape(micro * seq, head), g[:, :, columns].reshape(micro * seq, part), 0, 0
        )
        total[:, columns] = value
        if i < items:

            @pl.when(z == 0)
            def _():
                rs[i] = value.astype(jnp.bfloat16)
                r_copy(i).start()

            @pl.when(z == n - 1)
            def _():
                ls[i] = value.astype(jnp.bfloat16)
                l_copy(i).start()

    for i in range(PARTS):
        product(i)

    loads[2].wait()
    loads[3].wait()

    @pl.when(p > 0)
    def _():
        chosen = [plan_ref[0, j] for j in range(BMICRO)]
        acc = jnp.zeros((BMICRO * seq, head), jnp.float32)
        for k in range(PIECES):
            columns = pl.ds(k * width, width)
            lhs = jnp.concatenate([g[m, :, columns] for m in chosen], axis=0)
            acc = acc + mm(lhs, wo[columns, :], 1, 0)
        heads = []
        for j in range(BMICRO):
            m = chosen[j]
            grad_head = acc[j * seq : (j + 1) * seq].astype(jnp.bfloat16)
            softmax = probs[m]
            soft_low = softmax.astype(jnp.bfloat16)
            row_dot = jnp.sum(
                grad_head.astype(jnp.float32) * att[m].astype(jnp.float32), axis=1, keepdims=True
            )
            grad_values = mm(soft_low, grad_head, 0, 0)
            grad_probs = mm(grad_head, qkv[m, :, 2 * head :], 1, 1)
            grad_scores = (softmax * (grad_probs - row_dot)).astype(jnp.bfloat16)
            grad_query = mm(grad_scores, qkv[m, :, head : 2 * head], 1, 0) * scale
            grad_keys = mm(grad_scores, qkv[m, :, :head], 0, 0) * scale
            heads.append(jnp.concatenate([grad_query, grad_keys, grad_values], axis=1).astype(jnp.bfloat16))
        row = lax.broadcasted_iota(jnp.int32, (2 * rows, 2 * rows), 0)
        column = lax.broadcasted_iota(jnp.int32, (2 * rows, 2 * rows), 1)
        second = (row >= rows).astype(jnp.int32)
        side = second * x + (1 - second) * (1 - x)
        inner = row - second * rows
        token = lax.shift_right_logical(inner, 1)
        source = (inner - 2 * token) * seq + side * half + token
        order = (column == source).astype(jnp.bfloat16)
        gqkv[...] = mm(order, jnp.concatenate(heads, axis=0), 1, 0).astype(jnp.bfloat16)
        for k in FAR + NEAR:
            term = mm(gqkv[...], wq[pl.ds(k * width, width), :], 1, 1).astype(jnp.bfloat16)
            xs[k] = term[:rows]
            own[k] = term[rows:]
            if k in FAR:

                @pl.when(p == 2)
                def _():
                    f_copy(k).start()
                    h_copy(k).start()

                @pl.when(p != 2)
                def _():
                    x_copy(k).start()

            else:
                x_copy(k).start()

    for i in range(PARTS, items + PARTS):
        product(i)

    @pl.when(p == sections - 1)
    def _():
        in_ref[...] = jnp.zeros_like(in_ref)

    def summed(mine, other):
        value = mine.astype(jnp.float32) + other.astype(jnp.float32)
        return value.reshape(half, BMICRO, width).astype(jnp.bfloat16)

    def do_x(k):
        x_copy(k).wait_recv()
        ys[k] = summed(own[k], xr[k])
        y_copy(k).start()

    def do_odd(k):
        @pl.when((p == 1) | (p == 3))
        def _():
            do_x(k)

    def do_two(k):
        @pl.when(p == 2)
        def _():
            do_x(k)

    def pass_on(k):
        @pl.when(p == 1)
        def _():
            f_copy(k).wait_recv()
            o_copy(k).start()

    def finish(k):
        @pl.when(p == 1)
        def _():
            h_copy(k).wait_recv()
            o_copy(k).wait_recv()
            in_ref[:, :, pl.ds(k * width, width)] = summed(hr[k // 2], fo[k // 2])

    def do_z(i):
        right_chunk = n - 1 - i // PARTS
        left_chunk = i // PARTS
        right_cols, left_cols = r_columns(i), l_columns(i)

        @pl.when((z > 0) & (z < right_chunk))
        def _():
            r_copy(i).wait_recv()
            rs[i] = (total[:, right_cols] + rr[i].astype(jnp.float32)).astype(jnp.bfloat16)
            r_copy(i).start()

        @pl.when((z < n - 1) & (z > left_chunk))
        def _():
            l_copy(i).wait_recv()
            ls[i] = (total[:, left_cols] + lr[i].astype(jnp.float32)).astype(jnp.bfloat16)
            l_copy(i).start()

        @pl.when(z == right_chunk)
        def _():
            r_copy(i).wait_recv()
            total[:, right_cols] = total[:, right_cols] + rr[i].astype(jnp.float32)

        @pl.when(z == left_chunk)
        def _():
            l_copy(i).wait_recv()
            total[:, left_cols] = total[:, left_cols] + lr[i].astype(jnp.float32)

    events = [(5.0 + 26.0 * (i + 1) / items, do_z, i) for i in range(items)]
    events += [(8.5 + 2.4 * (i + 1), do_odd, k) for i, k in enumerate(FAR + NEAR)]
    events += [(8.5 + 3.6 * (i + 1), do_two, k) for i, k in enumerate(NEAR)]
    events += [(10.5 + 3.6 * i, pass_on, k) for i, k in enumerate(FAR)]
    events += [(29.0 + i, finish, k) for i, k in enumerate(FAR)]
    for _, act, index in sorted(events, key=lambda e: e[0]):
        act(index)

    for i in range(PARTS):
        columns = pl.ds(pl.multiple_of(z * chunk + i * part, part), part)
        wg_ref[i * part : (i + 1) * part, :] = total[:, columns].T

    @pl.when(p < sections - 1)
    def _():
        for k in NEAR:
            y_copy(k).wait_recv()

    @pl.when((p == 0) | (p == 2))
    def _():
        for k in FAR:
            y_copy(k).wait_recv()

    @pl.when(p > 0)
    def _():
        for k in NEAR:
            x_copy(k).wait_send()
            y_copy(k).wait_send()

    @pl.when((p == 1) | (p == 3))
    def _():
        for k in FAR:
            x_copy(k).wait_send()
            y_copy(k).wait_send()

    @pl.when(p == 2)
    def _():
        for k in FAR:
            f_copy(k).wait_send()
            h_copy(k).wait_send()

    @pl.when(p == 1)
    def _():
        for k in FAR:
            o_copy(k).wait_send()

    for i in range(items):

        @pl.when(z < n - 1 - i // PARTS)
        def _():
            r_copy(i).wait_send()

        @pl.when(z > i // PARTS)
        def _():
            l_copy(i).wait_send()


def fused_body(n, sections, grad_out, qkv_saved, w_out, w_qkv, plan):
    _, micro, _, seq, features = grad_out.shape
    head = w_out.shape[-1]
    half = seq // 2
    rows = BMICRO * half
    width = features // PIECES
    part = features // n // PARTS
    items = (n - 1) * PARTS
    low, full = jnp.bfloat16, jnp.float32
    dma = pltpu.SemaphoreType.DMA
    strip = (items, head, part)
    term = (PIECES, rows, width)
    anywhere = pl.BlockSpec(memory_space=pl.ANY)
    vmem = pl.BlockSpec(memory_space=pltpu.VMEM)
    received, weight_grad = pl.pallas_call(
        functools.partial(fused_kernel, (n, sections, micro, seq, head, features)),
        out_shape=(
            jax.ShapeDtypeStruct((half, BMICRO, features), low),
            jax.ShapeDtypeStruct((features // n, head), full),
        ),
        in_specs=[pl.BlockSpec(memory_space=pltpu.SMEM)] + [anywhere] * 4,
        out_specs=(vmem, vmem),
        scratch_shapes=[
            pltpu.VMEM((micro, seq, features), low),
            pltpu.VMEM((micro, seq, 3 * head), low),
            pltpu.VMEM((features, head), low),
            pltpu.VMEM((features, 3 * head), low),
            pltpu.VMEM((micro, seq, seq), full),
            pltpu.VMEM((micro, seq, head), low),
            pltpu.VMEM((2 * rows, 3 * head), low),
            pltpu.VMEM((head, features), full),
        ]
        + [pltpu.VMEM(term, low)] * 3
        + [pltpu.VMEM((len(FAR), rows, width), low)] * 3
        + [pltpu.VMEM((PIECES, half, BMICRO, width), low)]
        + [pltpu.VMEM(strip, low)] * 4
        + [dma((4,))]
        + [dma((PIECES,))] * 4
        + [dma((len(FAR),))] * 6
        + [dma((items,))] * 4,
        compiler_params=pltpu.CompilerParams(
            collective_id=0, has_side_effects=True, vmem_limit_bytes=56 * 1024 * 1024
        ),
        cost_estimate=pl.CostEstimate(flops=2_000_000_000, bytes_accessed=14_000_000, transcendentals=40_000),
    )(
        plan,
        grad_out.reshape(micro, seq, features),
        qkv_saved.reshape(micro, seq, 3 * head),
        w_out.reshape(features, head),
        w_qkv.reshape(features, 3 * head),
    )
    return (received[None, None], weight_grad[None, :, None, :])


def solution(mesh):
    in_specs = (
        P("pipe", None, "dp", None, None),
        P("pipe", None, "dp", None, "tensor", None),
        P("pipe", None, "tensor", None),
        P("pipe", None, "tensor", None),
        P("pipe", None),
    )
    out_specs = (P("pipe", "dp", "tensor", None, None), P("pipe", "dp", "tensor", None))
    chosen = body
    if (mesh.shape["pipe"], mesh.shape["dp"], mesh.shape["tensor"]) == (4, 4, 2):
        chosen = functools.partial(fused_body, mesh.shape["dp"], mesh.shape["pipe"])
    return jax.shard_map(chosen, mesh=mesh, in_specs=in_specs, out_specs=out_specs, check_vma=False)
```

```python
import functools

import jax
import jax.numpy as jnp
from jax import lax
from jax.experimental import pallas as pl
from jax.experimental.pallas import tpu as pltpu
from jax.sharding import PartitionSpec as P

BMICRO = 2
PIECES = 8
FAR = [0, 2, 4, 6]
NEAR = [1, 3, 5, 7]
ORDER = [1, 0, 3, 2, 5, 4, 7, 6]
PARTS = 2
MESH = pl.DeviceIdType.MESH


def shifted(block, axis, distance):
    devices = range(lax.axis_size(axis))
    route = [(i - distance, i) for i in devices if i - distance in devices]
    return lax.ppermute(block, axis, route)


def head_forward(queries, key_rows, values):
    score_scale = queries.shape[-1] ** (-0.5)
    scores = jnp.dot(queries, key_rows.T, preferred_element_type=jnp.float32) * score_scale
    row_ids = lax.broadcasted_iota(jnp.int32, scores.shape, 0)
    col_ids = lax.broadcasted_iota(jnp.int32, scores.shape, 1)
    scores = jnp.where(col_ids <= row_ids, scores, -1e30)
    row_max = jnp.max(scores, axis=1, keepdims=True)
    weights = jnp.exp(scores - row_max)
    softmax = weights / jnp.sum(weights, axis=1, keepdims=True)
    soft_low = softmax.astype(jnp.bfloat16)
    attended = jnp.dot(soft_low, values, preferred_element_type=jnp.float32).astype(jnp.bfloat16)
    return (softmax, soft_low, attended)


def head_backward(queries, key_rows, values, softmax, soft_low, attended, grad_head):
    score_scale = queries.shape[-1] ** (-0.5)
    row_dot = jnp.sum(
        grad_head.astype(jnp.float32) * attended.astype(jnp.float32), axis=1, keepdims=True
    )
    grad_values = jnp.dot(soft_low.T, grad_head, preferred_element_type=jnp.float32)
    grad_probs = jnp.dot(grad_head, values.T, preferred_element_type=jnp.float32)
    grad_scores = (softmax * (grad_probs - row_dot)).astype(jnp.bfloat16)
    grad_query = jnp.dot(grad_scores, key_rows, preferred_element_type=jnp.float32) * score_scale
    grad_keys = jnp.dot(grad_scores.T, queries, preferred_element_type=jnp.float32) * score_scale
    return jnp.concatenate([grad_query, grad_keys, grad_values], axis=1).astype(jnp.bfloat16)


def body(grad_out, qkv_saved, w_out, w_qkv, plan):
    gradients = grad_out[0, :, 0]
    saved_qkv = qkv_saved[0, :, 0, :, 0]
    out_proj = w_out[0, :, 0]
    qkv_proj = w_qkv[0, :, 0]
    head_size = out_proj.shape[1]
    seq_len = gradients.shape[1]
    queries = saved_qkv[:, :, :head_size]
    key_rows = saved_qkv[:, :, head_size : 2 * head_size]
    values = saved_qkv[:, :, 2 * head_size :]
    softmax, soft_low, attended = jax.vmap(head_forward)(queries, key_rows, values)
    current = plan[0, :BMICRO]
    grad_current = jnp.take(gradients, current, axis=0)
    grad_heads = jnp.einsum(
        "msd,dh->msh", grad_current, out_proj, preferred_element_type=jnp.float32
    ).astype(jnp.bfloat16)
    grad_qkv = jax.vmap(head_backward)(
        jnp.take(queries, current, axis=0),
        jnp.take(key_rows, current, axis=0),
        jnp.take(values, current, axis=0),
        jnp.take(softmax, current, axis=0),
        jnp.take(soft_low, current, axis=0),
        jnp.take(attended, current, axis=0),
        grad_heads,
    )
    share_rows = seq_len // lax.axis_size("tensor")
    partials = jnp.einsum("bsk,dk->sbd", grad_qkv, qkv_proj, preferred_element_type=jnp.float32)
    summed = lax.psum(partials.astype(jnp.bfloat16), "tensor").astype(jnp.float32)
    own_rows = lax.dynamic_slice_in_dim(
        summed, lax.axis_index("tensor") * share_rows, share_rows, 0
    )
    received = shifted(own_rows.astype(jnp.bfloat16), "pipe", -1)
    weight_grad = lax.psum_scatter(
        jnp.einsum("msc,msh->ch", gradients, attended, preferred_element_type=jnp.float32),
        "dp",
        scatter_dimension=0,
        tiled=True,
    )
    return (received[None, None], weight_grad[None, :, None, :])


def mm(left, right, left_dim, right_dim):
    return lax.dot_general(
        left, right, (((left_dim,), (right_dim,)), ((), ())), preferred_element_type=jnp.float32
    )


def fused_kernel(
    sizes, plan_ref, g_hbm, qkv_hbm, wo_hbm, wq_hbm, in_ref, wg_ref,
    g, qkv, wo, wq, probs, att, gqkv, total, xs, own, xr, fr, hr, fo, ys, rs, rr, ls, lr,
    load_sem, x_send, x_recv, y_send, y_recv, f_send, f_recv, h_send, h_recv, o_send, o_recv, r_send, r_recv, l_send, l_recv,
):
    n, sections, micro, seq, head, features = sizes
    p = lax.axis_index("pipe")
    z = lax.axis_index("dp")
    x = lax.axis_index("tensor")
    scale = head ** (-0.5)
    half = seq // 2
    rows = BMICRO * half
    width = features // PIECES
    chunk = features // n
    part = chunk // PARTS
    items = (n - 1) * PARTS

    loads = [
        pltpu.make_async_copy(src, dst, load_sem.at[i])
        for i, (src, dst) in enumerate(((qkv_hbm, qkv), (g_hbm, g), (wo_hbm, wo), (wq_hbm, wq)))
    ]
    loads[0].start()
    loads[1].start()

    barrier = pltpu.get_barrier_semaphore()

    def greet(target):
        pl.semaphore_signal(barrier, inc=1, device_id=target, device_id_type=MESH)

    @pl.when(z > 0)
    def _():
        greet({"dp": z - 1})

    @pl.when(z < n - 1)
    def _():
        greet({"dp": z + 1})

    @pl.when(p > 0)
    def _():
        greet({"tensor": 1 - x})

    @pl.when(p < sections - 1)
    def _():
        greet({"pipe": p + 1})

    def x_copy(k):
        return pltpu.make_async_remote_copy(
            src_ref=xs.at[k], dst_ref=xr.at[k], send_sem=x_send.at[k], recv_sem=x_recv.at[k],
            device_id={"tensor": 1 - x}, device_id_type=MESH,
        )

    def y_copy(k):
        return pltpu.make_async_remote_copy(
            src_ref=ys.at[k], dst_ref=in_ref.at[:, :, pl.ds(k * width, width)],
            send_sem=y_send.at[k], recv_sem=y_recv.at[k],
            device_id={"pipe": p - 1}, device_id_type=MESH,
        )

    def f_copy(k):
        return pltpu.make_async_remote_copy(
            src_ref=xs.at[k], dst_ref=fr.at[k // 2], send_sem=f_send.at[k // 2], recv_sem=f_recv.at[k // 2],
            device_id={"pipe": p - 1}, device_id_type=MESH,
        )

    def h_copy(k):
        return pltpu.make_async_remote_copy(
            src_ref=own.at[k], dst_ref=hr.at[k // 2], send_sem=h_send.at[k // 2], recv_sem=h_recv.at[k // 2],
            device_id={"pipe": p - 1}, device_id_type=MESH,
        )

    def o_copy(k):
        return pltpu.make_async_remote_copy(
            src_ref=fr.at[k // 2], dst_ref=fo.at[k // 2], send_sem=o_send.at[k // 2], recv_sem=o_recv.at[k // 2],
            device_id={"tensor": 1 - x}, device_id_type=MESH,
        )

    def r_copy(i):
        return pltpu.make_async_remote_copy(
            src_ref=rs.at[i], dst_ref=rr.at[i], send_sem=r_send.at[i], recv_sem=r_recv.at[i],
            device_id={"dp": z + 1}, device_id_type=MESH,
        )

    def l_copy(i):
        return pltpu.make_async_remote_copy(
            src_ref=ls.at[i], dst_ref=lr.at[i], send_sem=l_send.at[i], recv_sem=l_recv.at[i],
            device_id={"dp": z - 1}, device_id_type=MESH,
        )

    def r_columns(i):
        return pl.ds((n - 1 - i // PARTS) * chunk + (i % PARTS) * part, part)

    def l_columns(i):
        return pl.ds((i // PARTS) * chunk + (i % PARTS) * part, part)

    loads[0].wait()
    keep = lax.broadcasted_iota(jnp.int32, (seq, seq), 1) <= lax.broadcasted_iota(jnp.int32, (seq, seq), 0)
    softs = []
    for m in range(micro):
        scores = mm(qkv[m, :, :head], qkv[m, :, head : 2 * head], 1, 1) * scale
        scores = jnp.where(keep, scores, -1e30)
        weights = jnp.exp(scores - jnp.max(scores, axis=1, keepdims=True))
        softs.append(weights / jnp.sum(weights, axis=1, keepdims=True))
    outs = [
        mm(softs[m].astype(jnp.bfloat16), qkv[m, :, 2 * head :], 1, 0).astype(jnp.bfloat16)
        for m in range(micro)
    ]
    for m in range(micro):
        probs[m] = softs[m]
        att[m] = outs[m]
    loads[2].start()
    loads[3].start()

    peers = lax.div(z + n - 1, n) + lax.div(2 * n - 2 - z, n) + 2 * lax.div(p + sections - 1, sections)
    pl.semaphore_wait(barrier, peers)

    loads[1].wait()

    upper = lax.div(z, n // 2)

    def product(i):
        place = upper * (i // PARTS) + (1 - upper) * (n - 1 - i // PARTS)
        columns = pl.ds(pl.multiple_of(place * chunk + (i % PARTS) * part, part), part)
        value = mm(
            att[...].reshape(micro * seq, head), g[:, :, columns].reshape(micro * seq, part), 0, 0
        )
        total[:, columns] = value
        if i < items:

            @pl.when(z == 0)
            def _():
                rs[i] = value.astype(jnp.bfloat16)
                r_copy(i).start()

            @pl.when(z == n - 1)
            def _():
                ls[i] = value.astype(jnp.bfloat16)
                l_copy(i).start()

    for i in range(PARTS):
        product(i)

    loads[2].wait()
    loads[3].wait()

    @pl.when(p > 0)
    def _():
        chosen = [plan_ref[0, j] for j in range(BMICRO)]
        acc = jnp.zeros((BMICRO * seq, head), jnp.float32)
        for k in range(PIECES):
            columns = pl.ds(k * width, width)
            lhs = jnp.concatenate([g[m, :, columns] for m in chosen], axis=0)
            acc = acc + mm(lhs, wo[columns, :], 1, 0)
        heads = []
        for j in range(BMICRO):
            m = chosen[j]
            grad_head = acc[j * seq : (j + 1) * seq].astype(jnp.bfloat16)
            softmax = probs[m]
            soft_low = softmax.astype(jnp.bfloat16)
            row_dot = jnp.sum(
                grad_head.astype(jnp.float32) * att[m].astype(jnp.float32), axis=1, keepdims=True
            )
            grad_values = mm(soft_low, grad_head, 0, 0)
            grad_probs = mm(grad_head, qkv[m, :, 2 * head :], 1, 1)
            grad_scores = (softmax * (grad_probs - row_dot)).astype(jnp.bfloat16)
            grad_query = mm(grad_scores, qkv[m, :, head : 2 * head], 1, 0) * scale
            grad_keys = mm(grad_scores, qkv[m, :, :head], 0, 0) * scale
            heads.append(jnp.concatenate([grad_query, grad_keys, grad_values], axis=1).astype(jnp.bfloat16))
        row = lax.broadcasted_iota(jnp.int32, (2 * rows, 2 * rows), 0)
        column = lax.broadcasted_iota(jnp.int32, (2 * rows, 2 * rows), 1)
        second = (row >= rows).astype(jnp.int32)
        side = second * x + (1 - second) * (1 - x)
        inner = row - second * rows
        token = lax.shift_right_logical(inner, 1)
        source = (inner - 2 * token) * seq + side * half + token
        order = (column == source).astype(jnp.bfloat16)
        gqkv[...] = mm(order, jnp.concatenate(heads, axis=0), 1, 0).astype(jnp.bfloat16)
        for k in ORDER:
            term = mm(gqkv[...], wq[pl.ds(k * width, width), :], 1, 1).astype(jnp.bfloat16)
            xs[k] = term[:rows]
            own[k] = term[rows:]
            if k in FAR:

                @pl.when(p == 2)
                def _():
                    f_copy(k).start()

                @pl.when(p != 2)
                def _():
                    x_copy(k).start()

            else:
                x_copy(k).start()

        @pl.when(p == 2)
        def _():
            for k in FAR:
                h_copy(k).start()

    for i in range(PARTS, items + PARTS):
        product(i)

    @pl.when(p == sections - 1)
    def _():
        in_ref[...] = jnp.zeros_like(in_ref)

    def summed(mine, other):
        value = mine.astype(jnp.float32) + other.astype(jnp.float32)
        return value.reshape(half, BMICRO, width).astype(jnp.bfloat16)

    def do_x(k):
        x_copy(k).wait_recv()
        ys[k] = summed(own[k], xr[k])
        y_copy(k).start()

    def do_odd(k):
        @pl.when((p == 1) | (p == 3))
        def _():
            do_x(k)

    def do_two(k):
        @pl.when(p == 2)
        def _():
            do_x(k)

    def pass_on(k):
        @pl.when(p == 1)
        def _():
            f_copy(k).wait_recv()
            o_copy(k).start()

    def finish(k):
        @pl.when(p == 1)
        def _():
            h_copy(k).wait_recv()
            o_copy(k).wait_recv()
            in_ref[:, :, pl.ds(k * width, width)] = summed(hr[k // 2], fo[k // 2])

    def do_z(i):
        right_chunk = n - 1 - i // PARTS
        left_chunk = i // PARTS
        right_cols, left_cols = r_columns(i), l_columns(i)

        @pl.when((z > 0) & (z < right_chunk))
        def _():
            r_copy(i).wait_recv()
            rs[i] = (total[:, right_cols] + rr[i].astype(jnp.float32)).astype(jnp.bfloat16)
            r_copy(i).start()

        @pl.when((z < n - 1) & (z > left_chunk))
        def _():
            l_copy(i).wait_recv()
            ls[i] = (total[:, left_cols] + lr[i].astype(jnp.float32)).astype(jnp.bfloat16)
            l_copy(i).start()

        @pl.when(z == right_chunk)
        def _():
            r_copy(i).wait_recv()
            total[:, right_cols] = total[:, right_cols] + rr[i].astype(jnp.float32)

        @pl.when(z == left_chunk)
        def _():
            l_copy(i).wait_recv()
            total[:, left_cols] = total[:, left_cols] + lr[i].astype(jnp.float32)

    events = [(5.0 + 26.0 * (i + 1) / items, do_z, i) for i in range(items)]
    events += [(8.5 + 2.4 * (i + 1), do_odd, k) for i, k in enumerate(ORDER)]
    events += [(8.5 + 3.6 * (i + 1), do_two, k) for i, k in enumerate(NEAR)]
    events += [(10.5 + 3.6 * i, pass_on, k) for i, k in enumerate(FAR)]
    events += [(29.0 + i, finish, k) for i, k in enumerate(FAR)]
    for _, act, index in sorted(events, key=lambda e: e[0]):
        act(index)

    for i in range(PARTS):
        columns = pl.ds(pl.multiple_of(z * chunk + i * part, part), part)
        wg_ref[i * part : (i + 1) * part, :] = total[:, columns].T

    @pl.when(p < sections - 1)
    def _():
        for k in NEAR:
            y_copy(k).wait_recv()

    @pl.when((p == 0) | (p == 2))
    def _():
        for k in FAR:
            y_copy(k).wait_recv()

    @pl.when(p > 0)
    def _():
        for k in NEAR:
            x_copy(k).wait_send()
            y_copy(k).wait_send()

    @pl.when((p == 1) | (p == 3))
    def _():
        for k in FAR:
            x_copy(k).wait_send()
            y_copy(k).wait_send()

    @pl.when(p == 2)
    def _():
        for k in FAR:
            f_copy(k).wait_send()
            h_copy(k).wait_send()

    @pl.when(p == 1)
    def _():
        for k in FAR:
            o_copy(k).wait_send()

    for i in range(items):

        @pl.when(z < n - 1 - i // PARTS)
        def _():
            r_copy(i).wait_send()

        @pl.when(z > i // PARTS)
        def _():
            l_copy(i).wait_send()


def copy_kernel(in_from, wg_from, in_to, wg_to, sem):
    tokens, rows = in_from.shape[0] // 4, wg_from.shape[0] // 4
    copies = []
    for i in range(4):
        cut = pl.ds(i * tokens, tokens)
        copies.append(pltpu.make_async_copy(in_from.at[cut], in_to.at[cut], sem.at[i]))
        cut = pl.ds(i * rows, rows)
        copies.append(pltpu.make_async_copy(wg_from.at[cut], wg_to.at[cut], sem.at[4 + i]))
    for copy in copies:
        copy.start()
    for copy in copies:
        copy.wait()


def fused_body(n, sections, grad_out, qkv_saved, w_out, w_qkv, plan):
    _, micro, _, seq, features = grad_out.shape
    head = w_out.shape[-1]
    half = seq // 2
    rows = BMICRO * half
    width = features // PIECES
    part = features // n // PARTS
    items = (n - 1) * PARTS
    low, full = jnp.bfloat16, jnp.float32
    dma = pltpu.SemaphoreType.DMA
    strip = (items, head, part)
    term = (PIECES, rows, width)
    anywhere = pl.BlockSpec(memory_space=pl.ANY)
    vmem = pl.BlockSpec(memory_space=pltpu.VMEM)
    received, weight_grad = pl.pallas_call(
        functools.partial(fused_kernel, (n, sections, micro, seq, head, features)),
        out_shape=(
            jax.ShapeDtypeStruct((half, BMICRO, features), low),
            jax.ShapeDtypeStruct((features // n, head), full),
        ),
        in_specs=[pl.BlockSpec(memory_space=pltpu.SMEM)] + [anywhere] * 4,
        out_specs=(vmem, vmem),
        scratch_shapes=[
            pltpu.VMEM((micro, seq, features), low),
            pltpu.VMEM((micro, seq, 3 * head), low),
            pltpu.VMEM((features, head), low),
            pltpu.VMEM((features, 3 * head), low),
            pltpu.VMEM((micro, seq, seq), full),
            pltpu.VMEM((micro, seq, head), low),
            pltpu.VMEM((2 * rows, 3 * head), low),
            pltpu.VMEM((head, features), full),
        ]
        + [pltpu.VMEM(term, low)] * 3
        + [pltpu.VMEM((len(FAR), rows, width), low)] * 3
        + [pltpu.VMEM((PIECES, half, BMICRO, width), low)]
        + [pltpu.VMEM(strip, low)] * 4
        + [dma((4,))]
        + [dma((PIECES,))] * 4
        + [dma((len(FAR),))] * 6
        + [dma((items,))] * 4,
        compiler_params=pltpu.CompilerParams(
            collective_id=0, has_side_effects=True, vmem_limit_bytes=56 * 1024 * 1024
        ),
        cost_estimate=pl.CostEstimate(flops=2_000_000_000, bytes_accessed=14_000_000, transcendentals=40_000),
    )(
        plan,
        grad_out.reshape(micro, seq, features),
        qkv_saved.reshape(micro, seq, 3 * head),
        w_out.reshape(features, head),
        w_qkv.reshape(features, 3 * head),
    )
    received, weight_grad = pl.pallas_call(
        copy_kernel,
        out_shape=(
            jax.ShapeDtypeStruct(received.shape, low),
            jax.ShapeDtypeStruct(weight_grad.shape, full),
        ),
        in_specs=[anywhere] * 2,
        out_specs=(anywhere, anywhere),
        scratch_shapes=[dma((8,))],
        compiler_params=pltpu.CompilerParams(vmem_limit_bytes=63 * 1024 * 1024),
    )(received, weight_grad)
    return (received[None, None], weight_grad[None, :, None, :])


def solution(mesh):
    in_specs = (
        P("pipe", None, "dp", None, None),
        P("pipe", None, "dp", None, "tensor", None),
        P("pipe", None, "tensor", None),
        P("pipe", None, "tensor", None),
        P("pipe", None),
    )
    out_specs = (P("pipe", "dp", "tensor", None, None), P("pipe", "dp", "tensor", None))
    chosen = body
    if (mesh.shape["pipe"], mesh.shape["dp"], mesh.shape["tensor"]) == (4, 4, 2):
        chosen = functools.partial(fused_body, mesh.shape["dp"], mesh.shape["pipe"])
    return jax.shard_map(chosen, mesh=mesh, in_specs=in_specs, out_specs=out_specs, check_vma=False)
```

```python
import functools

import jax
import jax.numpy as jnp
from jax import lax
from jax.experimental import pallas as pl
from jax.experimental.pallas import tpu as pltpu
from jax.sharding import PartitionSpec as P

BMICRO = 2
PIECES = 8
FAR = [0, 2, 4, 6]
NEAR = [1, 3, 5, 7]
ORDER = [1, 0, 3, 2, 5, 4, 7, 6]
PARTS = 2
MESH = pl.DeviceIdType.MESH


def shifted(block, axis, distance):
    devices = range(lax.axis_size(axis))
    route = [(i - distance, i) for i in devices if i - distance in devices]
    return lax.ppermute(block, axis, route)


def head_forward(queries, key_rows, values):
    score_scale = queries.shape[-1] ** (-0.5)
    scores = jnp.dot(queries, key_rows.T, preferred_element_type=jnp.float32) * score_scale
    row_ids = lax.broadcasted_iota(jnp.int32, scores.shape, 0)
    col_ids = lax.broadcasted_iota(jnp.int32, scores.shape, 1)
    scores = jnp.where(col_ids <= row_ids, scores, -1e30)
    row_max = jnp.max(scores, axis=1, keepdims=True)
    weights = jnp.exp(scores - row_max)
    softmax = weights / jnp.sum(weights, axis=1, keepdims=True)
    soft_low = softmax.astype(jnp.bfloat16)
    attended = jnp.dot(soft_low, values, preferred_element_type=jnp.float32).astype(jnp.bfloat16)
    return (softmax, soft_low, attended)


def head_backward(queries, key_rows, values, softmax, soft_low, attended, grad_head):
    score_scale = queries.shape[-1] ** (-0.5)
    row_dot = jnp.sum(
        grad_head.astype(jnp.float32) * attended.astype(jnp.float32), axis=1, keepdims=True
    )
    grad_values = jnp.dot(soft_low.T, grad_head, preferred_element_type=jnp.float32)
    grad_probs = jnp.dot(grad_head, values.T, preferred_element_type=jnp.float32)
    grad_scores = (softmax * (grad_probs - row_dot)).astype(jnp.bfloat16)
    grad_query = jnp.dot(grad_scores, key_rows, preferred_element_type=jnp.float32) * score_scale
    grad_keys = jnp.dot(grad_scores.T, queries, preferred_element_type=jnp.float32) * score_scale
    return jnp.concatenate([grad_query, grad_keys, grad_values], axis=1).astype(jnp.bfloat16)


def body(grad_out, qkv_saved, w_out, w_qkv, plan):
    gradients = grad_out[0, :, 0]
    saved_qkv = qkv_saved[0, :, 0, :, 0]
    out_proj = w_out[0, :, 0]
    qkv_proj = w_qkv[0, :, 0]
    head_size = out_proj.shape[1]
    seq_len = gradients.shape[1]
    queries = saved_qkv[:, :, :head_size]
    key_rows = saved_qkv[:, :, head_size : 2 * head_size]
    values = saved_qkv[:, :, 2 * head_size :]
    softmax, soft_low, attended = jax.vmap(head_forward)(queries, key_rows, values)
    current = plan[0, :BMICRO]
    grad_current = jnp.take(gradients, current, axis=0)
    grad_heads = jnp.einsum(
        "msd,dh->msh", grad_current, out_proj, preferred_element_type=jnp.float32
    ).astype(jnp.bfloat16)
    grad_qkv = jax.vmap(head_backward)(
        jnp.take(queries, current, axis=0),
        jnp.take(key_rows, current, axis=0),
        jnp.take(values, current, axis=0),
        jnp.take(softmax, current, axis=0),
        jnp.take(soft_low, current, axis=0),
        jnp.take(attended, current, axis=0),
        grad_heads,
    )
    share_rows = seq_len // lax.axis_size("tensor")
    partials = jnp.einsum("bsk,dk->sbd", grad_qkv, qkv_proj, preferred_element_type=jnp.float32)
    summed = lax.psum(partials.astype(jnp.bfloat16), "tensor").astype(jnp.float32)
    own_rows = lax.dynamic_slice_in_dim(
        summed, lax.axis_index("tensor") * share_rows, share_rows, 0
    )
    received = shifted(own_rows.astype(jnp.bfloat16), "pipe", -1)
    weight_grad = lax.psum_scatter(
        jnp.einsum("msc,msh->ch", gradients, attended, preferred_element_type=jnp.float32),
        "dp",
        scatter_dimension=0,
        tiled=True,
    )
    return (received[None, None], weight_grad[None, :, None, :])


def mm(left, right, left_dim, right_dim):
    return lax.dot_general(
        left, right, (((left_dim,), (right_dim,)), ((), ())), preferred_element_type=jnp.float32
    )


def fused_kernel(
    sizes, plan_ref, g_hbm, qkv_hbm, wo_hbm, wq_hbm, in_ref, wg_ref,
    g, qkv, wo, wq, probs, att, att_t, gqkv, total, xs, own, xr, fr, hr, fo, ys, rs, rr, ls, lr,
    load_sem, x_send, x_recv, y_send, y_recv, f_send, f_recv, h_send, h_recv, o_send, o_recv, r_send, r_recv, l_send, l_recv,
):
    n, sections, micro, seq, head, features = sizes
    p = lax.axis_index("pipe")
    z = lax.axis_index("dp")
    x = lax.axis_index("tensor")
    scale = head ** (-0.5)
    half = seq // 2
    rows = BMICRO * half
    width = features // PIECES
    chunk = features // n
    part = chunk // PARTS
    items = (n - 1) * PARTS

    loads = [
        pltpu.make_async_copy(src, dst, load_sem.at[i])
        for i, (src, dst) in enumerate(((qkv_hbm, qkv), (g_hbm, g), (wo_hbm, wo), (wq_hbm, wq)))
    ]
    loads[0].start()
    loads[1].start()

    barrier = pltpu.get_barrier_semaphore()

    def greet(target):
        pl.semaphore_signal(barrier, inc=1, device_id=target, device_id_type=MESH)

    @pl.when(z > 0)
    def _():
        greet({"dp": z - 1})

    @pl.when(z < n - 1)
    def _():
        greet({"dp": z + 1})

    @pl.when(p > 0)
    def _():
        greet({"tensor": 1 - x})

    @pl.when(p < sections - 1)
    def _():
        greet({"pipe": p + 1})

    def x_copy(k):
        return pltpu.make_async_remote_copy(
            src_ref=xs.at[k], dst_ref=xr.at[k], send_sem=x_send.at[k], recv_sem=x_recv.at[k],
            device_id={"tensor": 1 - x}, device_id_type=MESH,
        )

    def y_copy(k):
        return pltpu.make_async_remote_copy(
            src_ref=ys.at[k], dst_ref=in_ref.at[:, :, pl.ds(k * width, width)],
            send_sem=y_send.at[k], recv_sem=y_recv.at[k],
            device_id={"pipe": p - 1}, device_id_type=MESH,
        )

    def f_copy(k):
        return pltpu.make_async_remote_copy(
            src_ref=xs.at[k], dst_ref=fr.at[k // 2], send_sem=f_send.at[k // 2], recv_sem=f_recv.at[k // 2],
            device_id={"pipe": p - 1}, device_id_type=MESH,
        )

    def h_copy(k):
        return pltpu.make_async_remote_copy(
            src_ref=own.at[k], dst_ref=hr.at[k // 2], send_sem=h_send.at[k // 2], recv_sem=h_recv.at[k // 2],
            device_id={"pipe": p - 1}, device_id_type=MESH,
        )

    def o_copy(k):
        return pltpu.make_async_remote_copy(
            src_ref=fr.at[k // 2], dst_ref=fo.at[k // 2], send_sem=o_send.at[k // 2], recv_sem=o_recv.at[k // 2],
            device_id={"tensor": 1 - x}, device_id_type=MESH,
        )

    def r_copy(i):
        return pltpu.make_async_remote_copy(
            src_ref=rs.at[i], dst_ref=rr.at[i], send_sem=r_send.at[i], recv_sem=r_recv.at[i],
            device_id={"dp": z + 1}, device_id_type=MESH,
        )

    def l_copy(i):
        return pltpu.make_async_remote_copy(
            src_ref=ls.at[i], dst_ref=lr.at[i], send_sem=l_send.at[i], recv_sem=l_recv.at[i],
            device_id={"dp": z - 1}, device_id_type=MESH,
        )

    def r_columns(i):
        return pl.ds((n - 1 - i // PARTS) * chunk + (i % PARTS) * part, part)

    def l_columns(i):
        return pl.ds((i // PARTS) * chunk + (i % PARTS) * part, part)

    loads[0].wait()
    keep = lax.broadcasted_iota(jnp.int32, (seq, seq), 1) <= lax.broadcasted_iota(jnp.int32, (seq, seq), 0)
    softs = []
    for m in range(micro):
        scores = mm(qkv[m, :, :head], qkv[m, :, head : 2 * head], 1, 1) * scale
        scores = jnp.where(keep, scores, -1e30)
        weights = jnp.exp(scores - jnp.max(scores, axis=1, keepdims=True))
        softs.append(weights / jnp.sum(weights, axis=1, keepdims=True))
    outs = [
        mm(softs[m].astype(jnp.bfloat16), qkv[m, :, 2 * head :], 1, 0).astype(jnp.bfloat16)
        for m in range(micro)
    ]
    for m in range(micro):
        probs[m] = softs[m]
        att[m] = outs[m]
    att_t[...] = jnp.concatenate(outs, axis=0).T
    loads[2].start()
    loads[3].start()

    peers = lax.div(z + n - 1, n) + lax.div(2 * n - 2 - z, n) + 2 * lax.div(p + sections - 1, sections)
    pl.semaphore_wait(barrier, peers)

    loads[1].wait()

    upper = lax.div(z, n // 2)

    def product(i):
        place = upper * (i // PARTS) + (1 - upper) * (n - 1 - i // PARTS)
        columns = pl.ds(pl.multiple_of(place * chunk + (i % PARTS) * part, part), part)
        value = mm(
            att_t[...], g[:, :, columns].reshape(micro * seq, part), 1, 0
        )
        total[:, columns] = value
        if i < items:

            @pl.when(z == 0)
            def _():
                rs[i] = value.astype(jnp.bfloat16)
                r_copy(i).start()

            @pl.when(z == n - 1)
            def _():
                ls[i] = value.astype(jnp.bfloat16)
                l_copy(i).start()

    for i in range(PARTS):
        product(i)

    @pl.when(p == 0)
    def _():
        loads[2].wait()
        loads[3].wait()

    @pl.when(p > 0)
    def _():
        loads[2].wait()
        chosen = [plan_ref[0, j] for j in range(BMICRO)]
        acc = jnp.zeros((BMICRO * seq, head), jnp.float32)
        for k in range(PIECES):
            columns = pl.ds(k * width, width)
            lhs = jnp.concatenate([g[m, :, columns] for m in chosen], axis=0)
            acc = acc + mm(lhs, wo[columns, :], 1, 0)
        heads = []
        for j in range(BMICRO):
            m = chosen[j]
            grad_head = acc[j * seq : (j + 1) * seq].astype(jnp.bfloat16)
            softmax = probs[m]
            soft_low = softmax.astype(jnp.bfloat16)
            row_dot = jnp.sum(
                grad_head.astype(jnp.float32) * att[m].astype(jnp.float32), axis=1, keepdims=True
            )
            grad_values = mm(soft_low, grad_head, 0, 0)
            grad_probs = mm(grad_head, qkv[m, :, 2 * head :], 1, 1)
            grad_scores = (softmax * (grad_probs - row_dot)).astype(jnp.bfloat16)
            grad_query = mm(grad_scores, qkv[m, :, head : 2 * head], 1, 0) * scale
            grad_keys = mm(grad_scores, qkv[m, :, :head], 0, 0) * scale
            heads.append(jnp.concatenate([grad_query, grad_keys, grad_values], axis=1).astype(jnp.bfloat16))
        row = lax.broadcasted_iota(jnp.int32, (2 * rows, 2 * rows), 0)
        column = lax.broadcasted_iota(jnp.int32, (2 * rows, 2 * rows), 1)
        second = (row >= rows).astype(jnp.int32)
        side = second * x + (1 - second) * (1 - x)
        inner = row - second * rows
        token = lax.shift_right_logical(inner, 1)
        source = (inner - 2 * token) * seq + side * half + token
        order = (column == source).astype(jnp.bfloat16)
        gqkv[...] = mm(order, jnp.concatenate(heads, axis=0), 1, 0).astype(jnp.bfloat16)
        loads[3].wait()
        for k in ORDER:
            term = mm(gqkv[...], wq[pl.ds(k * width, width), :], 1, 1).astype(jnp.bfloat16)
            xs[k] = term[:rows]
            own[k] = term[rows:]
            if k in FAR:

                @pl.when(p == 2)
                def _():
                    f_copy(k).start()

                @pl.when(p != 2)
                def _():
                    x_copy(k).start()

            else:
                x_copy(k).start()

        @pl.when(p == 2)
        def _():
            for k in FAR:
                h_copy(k).start()

    for i in range(PARTS, items + PARTS):
        product(i)

    @pl.when(p == sections - 1)
    def _():
        in_ref[...] = jnp.zeros_like(in_ref)

    def summed(mine, other):
        value = mine.astype(jnp.float32) + other.astype(jnp.float32)
        return value.reshape(half, BMICRO, width).astype(jnp.bfloat16)

    def do_x(k):
        x_copy(k).wait_recv()
        ys[k] = summed(own[k], xr[k])
        y_copy(k).start()

    def do_odd(k):
        @pl.when((p == 1) | (p == 3))
        def _():
            do_x(k)

    def do_two(k):
        @pl.when(p == 2)
        def _():
            do_x(k)

    def pass_on(k):
        @pl.when(p == 1)
        def _():
            f_copy(k).wait_recv()
            o_copy(k).start()

    def finish(k):
        @pl.when(p == 1)
        def _():
            h_copy(k).wait_recv()
            o_copy(k).wait_recv()
            in_ref[:, :, pl.ds(k * width, width)] = summed(hr[k // 2], fo[k // 2])

    def add_right(i, hop):
        place = n - 1 - i // PARTS
        columns = r_columns(i)

        @pl.when(z == hop + 1)
        def _():
            r_copy(i).wait_recv()
            value = total[:, columns] + rr[i].astype(jnp.float32)
            if hop + 1 < place:
                rs[i] = value.astype(jnp.bfloat16)
                r_copy(i).start()
            else:
                total[:, columns] = value

    def add_left(i, hop):
        place = i // PARTS
        columns = l_columns(i)

        @pl.when(z == n - 2 - hop)
        def _():
            l_copy(i).wait_recv()
            value = total[:, columns] + lr[i].astype(jnp.float32)
            if n - 2 - hop > place:
                ls[i] = value.astype(jnp.bfloat16)
                l_copy(i).start()
            else:
                total[:, columns] = value

    events = []
    for i in range(items):
        for hop in range(n - 1 - i // PARTS):
            due = 6.0 + 4.6 * (i + 1) + 3.5 * hop
            events.append((due, functools.partial(add_right, hop=hop), i))
            events.append((due, functools.partial(add_left, hop=hop), i))
    events += [(11.0 + 2.6 * (i + 1), do_odd, k) for i, k in enumerate(ORDER)]
    events += [(11.0 + 3.4 * (i + 1), do_two, k) for i, k in enumerate(NEAR)]
    events += [(10.0 + 3.4 * (i + 1), pass_on, k) for i, k in enumerate(FAR)]
    events += [(30.0 + i, finish, k) for i, k in enumerate(FAR)]
    for _, act, index in sorted(events, key=lambda e: e[0]):
        act(index)

    for i in range(PARTS):
        columns = pl.ds(pl.multiple_of(z * chunk + i * part, part), part)
        wg_ref[i * part : (i + 1) * part, :] = total[:, columns].T

    @pl.when(p < sections - 1)
    def _():
        for k in NEAR:
            y_copy(k).wait_recv()

    @pl.when((p == 0) | (p == 2))
    def _():
        for k in FAR:
            y_copy(k).wait_recv()

    @pl.when(p > 0)
    def _():
        for k in NEAR:
            x_copy(k).wait_send()
            y_copy(k).wait_send()

    @pl.when((p == 1) | (p == 3))
    def _():
        for k in FAR:
            x_copy(k).wait_send()
            y_copy(k).wait_send()

    @pl.when(p == 2)
    def _():
        for k in FAR:
            f_copy(k).wait_send()
            h_copy(k).wait_send()

    @pl.when(p == 1)
    def _():
        for k in FAR:
            o_copy(k).wait_send()

    for i in range(items):

        @pl.when(z < n - 1 - i // PARTS)
        def _():
            r_copy(i).wait_send()

        @pl.when(z > i // PARTS)
        def _():
            l_copy(i).wait_send()


def copy_kernel(in_from, wg_from, in_to, wg_to, in_mid, wg_mid, first, last):
    tokens, rows = in_from.shape[0] // 4, wg_from.shape[0] // 4
    arrive, leave = [], []
    for i in range(4):
        pairs = ((in_from, in_mid, in_to, tokens, i), (wg_from, wg_mid, wg_to, rows, 4 + i))
        for source, middle, target, size, slot in pairs:
            cut = pl.ds(i * size, size)
            arrive.append(pltpu.make_async_copy(source.at[cut], middle.at[cut], first.at[slot]))
            leave.append(pltpu.make_async_copy(middle.at[cut], target.at[cut], last.at[slot]))
    for copy in arrive:
        copy.start()
    for before, after in zip(arrive, leave):
        before.wait()
        after.start()
    for copy in leave:
        copy.wait()


def fused_body(n, sections, grad_out, qkv_saved, w_out, w_qkv, plan):
    _, micro, _, seq, features = grad_out.shape
    head = w_out.shape[-1]
    half = seq // 2
    rows = BMICRO * half
    width = features // PIECES
    part = features // n // PARTS
    items = (n - 1) * PARTS
    low, full = jnp.bfloat16, jnp.float32
    dma = pltpu.SemaphoreType.DMA
    strip = (items, head, part)
    term = (PIECES, rows, width)
    anywhere = pl.BlockSpec(memory_space=pl.ANY)
    vmem = pl.BlockSpec(memory_space=pltpu.VMEM)
    received, weight_grad = pl.pallas_call(
        functools.partial(fused_kernel, (n, sections, micro, seq, head, features)),
        out_shape=(
            jax.ShapeDtypeStruct((half, BMICRO, features), low),
            jax.ShapeDtypeStruct((features // n, head), full),
        ),
        in_specs=[pl.BlockSpec(memory_space=pltpu.SMEM)] + [anywhere] * 4,
        out_specs=(vmem, vmem),
        scratch_shapes=[
            pltpu.VMEM((micro, seq, features), low),
            pltpu.VMEM((micro, seq, 3 * head), low),
            pltpu.VMEM((features, head), low),
            pltpu.VMEM((features, 3 * head), low),
            pltpu.VMEM((micro, seq, seq), full),
            pltpu.VMEM((micro, seq, head), low),
            pltpu.VMEM((head, micro * seq), low),
            pltpu.VMEM((2 * rows, 3 * head), low),
            pltpu.VMEM((head, features), full),
        ]
        + [pltpu.VMEM(term, low)] * 3
        + [pltpu.VMEM((len(FAR), rows, width), low)] * 3
        + [pltpu.VMEM((PIECES, half, BMICRO, width), low)]
        + [pltpu.VMEM(strip, low)] * 4
        + [dma((4,))]
        + [dma((PIECES,))] * 4
        + [dma((len(FAR),))] * 6
        + [dma((items,))] * 4,
        compiler_params=pltpu.CompilerParams(
            collective_id=0, has_side_effects=True, vmem_limit_bytes=56 * 1024 * 1024
        ),
        cost_estimate=pl.CostEstimate(flops=2_000_000_000, bytes_accessed=14_000_000, transcendentals=40_000),
    )(
        plan,
        grad_out.reshape(micro, seq, features),
        qkv_saved.reshape(micro, seq, 3 * head),
        w_out.reshape(features, head),
        w_qkv.reshape(features, 3 * head),
    )
    received, weight_grad = pl.pallas_call(
        copy_kernel,
        out_shape=(
            jax.ShapeDtypeStruct(received.shape, low),
            jax.ShapeDtypeStruct(weight_grad.shape, full),
        ),
        in_specs=[anywhere] * 2,
        out_specs=(anywhere, anywhere),
        scratch_shapes=[
            pltpu.VMEM(received.shape, low),
            pltpu.VMEM(weight_grad.shape, full),
            dma((8,)),
            dma((8,)),
        ],
        compiler_params=pltpu.CompilerParams(vmem_limit_bytes=63 * 1024 * 1024),
    )(received, weight_grad)
    return (received[None, None], weight_grad[None, :, None, :])


def solution(mesh):
    in_specs = (
        P("pipe", None, "dp", None, None),
        P("pipe", None, "dp", None, "tensor", None),
        P("pipe", None, "tensor", None),
        P("pipe", None, "tensor", None),
        P("pipe", None),
    )
    out_specs = (P("pipe", "dp", "tensor", None, None), P("pipe", "dp", "tensor", None))
    chosen = body
    if (mesh.shape["pipe"], mesh.shape["dp"], mesh.shape["tensor"]) == (4, 4, 2):
        chosen = functools.partial(fused_body, mesh.shape["dp"], mesh.shape["pipe"])
    return jax.shard_map(chosen, mesh=mesh, in_specs=in_specs, out_specs=out_specs, check_vma=False)
```

```python
import functools

import jax
import jax.numpy as jnp
from jax import lax
from jax.experimental import pallas as pl
from jax.experimental.pallas import tpu as pltpu
from jax.sharding import PartitionSpec as P

BMICRO = 2
PIECES = 8
FAR = [0, 2, 4, 6]
NEAR = [1, 3, 5, 7]
ORDER = [1, 0, 3, 2, 5, 4, 7, 6]
PARTS = 4
MESH = pl.DeviceIdType.MESH


def shifted(block, axis, distance):
    devices = range(lax.axis_size(axis))
    route = [(i - distance, i) for i in devices if i - distance in devices]
    return lax.ppermute(block, axis, route)


def head_forward(queries, key_rows, values):
    score_scale = queries.shape[-1] ** (-0.5)
    scores = jnp.dot(queries, key_rows.T, preferred_element_type=jnp.float32) * score_scale
    row_ids = lax.broadcasted_iota(jnp.int32, scores.shape, 0)
    col_ids = lax.broadcasted_iota(jnp.int32, scores.shape, 1)
    scores = jnp.where(col_ids <= row_ids, scores, -1e30)
    row_max = jnp.max(scores, axis=1, keepdims=True)
    weights = jnp.exp(scores - row_max)
    softmax = weights / jnp.sum(weights, axis=1, keepdims=True)
    soft_low = softmax.astype(jnp.bfloat16)
    attended = jnp.dot(soft_low, values, preferred_element_type=jnp.float32).astype(jnp.bfloat16)
    return (softmax, soft_low, attended)


def head_backward(queries, key_rows, values, softmax, soft_low, attended, grad_head):
    score_scale = queries.shape[-1] ** (-0.5)
    row_dot = jnp.sum(
        grad_head.astype(jnp.float32) * attended.astype(jnp.float32), axis=1, keepdims=True
    )
    grad_values = jnp.dot(soft_low.T, grad_head, preferred_element_type=jnp.float32)
    grad_probs = jnp.dot(grad_head, values.T, preferred_element_type=jnp.float32)
    grad_scores = (softmax * (grad_probs - row_dot)).astype(jnp.bfloat16)
    grad_query = jnp.dot(grad_scores, key_rows, preferred_element_type=jnp.float32) * score_scale
    grad_keys = jnp.dot(grad_scores.T, queries, preferred_element_type=jnp.float32) * score_scale
    return jnp.concatenate([grad_query, grad_keys, grad_values], axis=1).astype(jnp.bfloat16)


def body(grad_out, qkv_saved, w_out, w_qkv, plan):
    gradients = grad_out[0, :, 0]
    saved_qkv = qkv_saved[0, :, 0, :, 0]
    out_proj = w_out[0, :, 0]
    qkv_proj = w_qkv[0, :, 0]
    head_size = out_proj.shape[1]
    seq_len = gradients.shape[1]
    queries = saved_qkv[:, :, :head_size]
    key_rows = saved_qkv[:, :, head_size : 2 * head_size]
    values = saved_qkv[:, :, 2 * head_size :]
    softmax, soft_low, attended = jax.vmap(head_forward)(queries, key_rows, values)
    current = plan[0, :BMICRO]
    grad_current = jnp.take(gradients, current, axis=0)
    grad_heads = jnp.einsum(
        "msd,dh->msh", grad_current, out_proj, preferred_element_type=jnp.float32
    ).astype(jnp.bfloat16)
    grad_qkv = jax.vmap(head_backward)(
        jnp.take(queries, current, axis=0),
        jnp.take(key_rows, current, axis=0),
        jnp.take(values, current, axis=0),
        jnp.take(softmax, current, axis=0),
        jnp.take(soft_low, current, axis=0),
        jnp.take(attended, current, axis=0),
        grad_heads,
    )
    share_rows = seq_len // lax.axis_size("tensor")
    partials = jnp.einsum("bsk,dk->sbd", grad_qkv, qkv_proj, preferred_element_type=jnp.float32)
    summed = lax.psum(partials.astype(jnp.bfloat16), "tensor").astype(jnp.float32)
    own_rows = lax.dynamic_slice_in_dim(
        summed, lax.axis_index("tensor") * share_rows, share_rows, 0
    )
    received = shifted(own_rows.astype(jnp.bfloat16), "pipe", -1)
    weight_grad = lax.psum_scatter(
        jnp.einsum("msc,msh->ch", gradients, attended, preferred_element_type=jnp.float32),
        "dp",
        scatter_dimension=0,
        tiled=True,
    )
    return (received[None, None], weight_grad[None, :, None, :])


def mm(left, right, left_dim, right_dim):
    return lax.dot_general(
        left, right, (((left_dim,), (right_dim,)), ((), ())), preferred_element_type=jnp.float32
    )


def fused_kernel(
    sizes, plan_ref, g_hbm, qkv_hbm, wo_hbm, wq_hbm, in_ref, wg_ref,
    g, qkv, wo, wq, probs, att, att_t, gqkv, total, xs, own, xr, fr, hr, fo, ys, rs, rr, ls, lr,
    load_sem, x_send, x_recv, y_send, y_recv, f_send, f_recv, h_send, h_recv, o_send, o_recv, r_send, r_recv, l_send, l_recv,
):
    n, sections, micro, seq, head, features = sizes
    p = lax.axis_index("pipe")
    z = lax.axis_index("dp")
    x = lax.axis_index("tensor")
    scale = head ** (-0.5)
    half = seq // 2
    rows = BMICRO * half
    width = features // PIECES
    chunk = features // n
    part = chunk // PARTS
    items = (n - 1) * PARTS

    loads = [
        pltpu.make_async_copy(src, dst, load_sem.at[i])
        for i, (src, dst) in enumerate(((qkv_hbm, qkv), (g_hbm, g), (wo_hbm, wo), (wq_hbm, wq)))
    ]
    loads[0].start()
    loads[1].start()

    barrier = pltpu.get_barrier_semaphore()

    def greet(target):
        pl.semaphore_signal(barrier, inc=1, device_id=target, device_id_type=MESH)

    @pl.when(z > 0)
    def _():
        greet({"dp": z - 1})

    @pl.when(z < n - 1)
    def _():
        greet({"dp": z + 1})

    @pl.when(p > 0)
    def _():
        greet({"tensor": 1 - x})

    @pl.when(p < sections - 1)
    def _():
        greet({"pipe": p + 1})

    def x_copy(k):
        return pltpu.make_async_remote_copy(
            src_ref=xs.at[k], dst_ref=xr.at[k], send_sem=x_send.at[k], recv_sem=x_recv.at[k],
            device_id={"tensor": 1 - x}, device_id_type=MESH,
        )

    def y_copy(k):
        return pltpu.make_async_remote_copy(
            src_ref=ys.at[k], dst_ref=in_ref.at[:, :, pl.ds(k * width, width)],
            send_sem=y_send.at[k], recv_sem=y_recv.at[k],
            device_id={"pipe": p - 1}, device_id_type=MESH,
        )

    def f_copy(k):
        return pltpu.make_async_remote_copy(
            src_ref=xs.at[k], dst_ref=fr.at[k // 2], send_sem=f_send.at[k // 2], recv_sem=f_recv.at[k // 2],
            device_id={"pipe": p - 1}, device_id_type=MESH,
        )

    def h_copy(k):
        return pltpu.make_async_remote_copy(
            src_ref=own.at[k], dst_ref=hr.at[k // 2], send_sem=h_send.at[k // 2], recv_sem=h_recv.at[k // 2],
            device_id={"pipe": p - 1}, device_id_type=MESH,
        )

    def o_copy(k):
        return pltpu.make_async_remote_copy(
            src_ref=fr.at[k // 2], dst_ref=fo.at[k // 2], send_sem=o_send.at[k // 2], recv_sem=o_recv.at[k // 2],
            device_id={"tensor": 1 - x}, device_id_type=MESH,
        )

    def r_copy(i):
        return pltpu.make_async_remote_copy(
            src_ref=rs.at[i], dst_ref=rr.at[i], send_sem=r_send.at[i], recv_sem=r_recv.at[i],
            device_id={"dp": z + 1}, device_id_type=MESH,
        )

    def l_copy(i):
        return pltpu.make_async_remote_copy(
            src_ref=ls.at[i], dst_ref=lr.at[i], send_sem=l_send.at[i], recv_sem=l_recv.at[i],
            device_id={"dp": z - 1}, device_id_type=MESH,
        )

    def r_columns(i):
        return pl.ds((n - 1 - i // PARTS) * chunk + (i % PARTS) * part, part)

    def l_columns(i):
        return pl.ds((i // PARTS) * chunk + (i % PARTS) * part, part)

    loads[0].wait()
    keep = lax.broadcasted_iota(jnp.int32, (seq, seq), 1) <= lax.broadcasted_iota(jnp.int32, (seq, seq), 0)
    softs = []
    for m in range(micro):
        scores = mm(qkv[m, :, :head], qkv[m, :, head : 2 * head], 1, 1) * scale
        scores = jnp.where(keep, scores, -1e30)
        weights = jnp.exp(scores - jnp.max(scores, axis=1, keepdims=True))
        softs.append(weights / jnp.sum(weights, axis=1, keepdims=True))
    outs = [
        mm(softs[m].astype(jnp.bfloat16), qkv[m, :, 2 * head :], 1, 0).astype(jnp.bfloat16)
        for m in range(micro)
    ]
    for m in range(micro):
        probs[m] = softs[m]
        att[m] = outs[m]
    att_t[...] = jnp.concatenate(outs, axis=0).T
    loads[2].start()
    loads[3].start()

    peers = lax.div(z + n - 1, n) + lax.div(2 * n - 2 - z, n) + 2 * lax.div(p + sections - 1, sections)
    pl.semaphore_wait(barrier, peers)

    loads[1].wait()

    upper = lax.div(z, n // 2)

    def product(i):
        place = upper * (i // PARTS) + (1 - upper) * (n - 1 - i // PARTS)
        columns = pl.ds(pl.multiple_of(place * chunk + (i % PARTS) * part, part), part)
        value = mm(
            att_t[...], g[:, :, columns].reshape(micro * seq, part), 1, 0
        )
        total[:, columns] = value
        if i < items:

            @pl.when(z == 0)
            def _():
                rs[i] = value.astype(jnp.bfloat16)
                r_copy(i).start()

            @pl.when(z == n - 1)
            def _():
                ls[i] = value.astype(jnp.bfloat16)
                l_copy(i).start()

    for i in range(PARTS + 2):
        product(i)

    @pl.when(p == 0)
    def _():
        loads[2].wait()
        loads[3].wait()

    @pl.when(p > 0)
    def _():
        loads[2].wait()
        chosen = [plan_ref[0, j] for j in range(BMICRO)]
        acc = jnp.zeros((BMICRO * seq, head), jnp.float32)
        for k in range(PIECES):
            columns = pl.ds(k * width, width)
            lhs = jnp.concatenate([g[m, :, columns] for m in chosen], axis=0)
            acc = acc + mm(lhs, wo[columns, :], 1, 0)
        heads = []
        for j in range(BMICRO):
            m = chosen[j]
            grad_head = acc[j * seq : (j + 1) * seq].astype(jnp.bfloat16)
            softmax = probs[m]
            soft_low = softmax.astype(jnp.bfloat16)
            row_dot = jnp.sum(
                grad_head.astype(jnp.float32) * att[m].astype(jnp.float32), axis=1, keepdims=True
            )
            grad_values = mm(soft_low, grad_head, 0, 0)
            grad_probs = mm(grad_head, qkv[m, :, 2 * head :], 1, 1)
            grad_scores = (softmax * (grad_probs - row_dot)).astype(jnp.bfloat16)
            grad_query = mm(grad_scores, qkv[m, :, head : 2 * head], 1, 0) * scale
            grad_keys = mm(grad_scores, qkv[m, :, :head], 0, 0) * scale
            heads.append(jnp.concatenate([grad_query, grad_keys, grad_values], axis=1).astype(jnp.bfloat16))
        row = lax.broadcasted_iota(jnp.int32, (2 * rows, 2 * rows), 0)
        column = lax.broadcasted_iota(jnp.int32, (2 * rows, 2 * rows), 1)
        second = (row >= rows).astype(jnp.int32)
        side = second * x + (1 - second) * (1 - x)
        inner = row - second * rows
        token = lax.shift_right_logical(inner, 1)
        source = (inner - 2 * token) * seq + side * half + token
        order = (column == source).astype(jnp.bfloat16)
        gqkv[...] = mm(order, jnp.concatenate(heads, axis=0), 1, 0).astype(jnp.bfloat16)
        loads[3].wait()
        for k in ORDER:
            term = mm(gqkv[...], wq[pl.ds(k * width, width), :], 1, 1).astype(jnp.bfloat16)
            xs[k] = term[:rows]
            own[k] = term[rows:]
            if k in FAR:

                @pl.when(p == 2)
                def _():
                    f_copy(k).start()

                @pl.when(p != 2)
                def _():
                    x_copy(k).start()

            else:
                x_copy(k).start()

        @pl.when(p == 2)
        def _():
            for k in FAR:
                h_copy(k).start()

    for i in range(PARTS + 2, items + PARTS):
        product(i)

    @pl.when(p == sections - 1)
    def _():
        in_ref[...] = jnp.zeros_like(in_ref)

    def summed(mine, other):
        value = mine.astype(jnp.float32) + other.astype(jnp.float32)
        return value.reshape(half, BMICRO, width).astype(jnp.bfloat16)

    def do_x(k):
        x_copy(k).wait_recv()
        ys[k] = summed(own[k], xr[k])
        y_copy(k).start()

    def do_odd(k):
        @pl.when((p == 1) | (p == 3))
        def _():
            do_x(k)

    def do_two(k):
        @pl.when(p == 2)
        def _():
            do_x(k)

    def pass_on(k):
        @pl.when(p == 1)
        def _():
            f_copy(k).wait_recv()
            o_copy(k).start()

    def finish(k):
        @pl.when(p == 1)
        def _():
            h_copy(k).wait_recv()
            o_copy(k).wait_recv()
            in_ref[:, :, pl.ds(k * width, width)] = summed(hr[k // 2], fo[k // 2])

    def add_right(i, hop):
        place = n - 1 - i // PARTS
        columns = r_columns(i)

        @pl.when(z == hop + 1)
        def _():
            r_copy(i).wait_recv()
            value = total[:, columns] + rr[i].astype(jnp.float32)
            if hop + 1 < place:
                rs[i] = value.astype(jnp.bfloat16)
                r_copy(i).start()
            elif place == n - 1 or place < n // 2:
                wg_ref[pl.ds((i % PARTS) * part, part), :] = value.T
            else:
                total[:, columns] = value

    def add_left(i, hop):
        place = i // PARTS
        columns = l_columns(i)

        @pl.when(z == n - 2 - hop)
        def _():
            l_copy(i).wait_recv()
            value = total[:, columns] + lr[i].astype(jnp.float32)
            if n - 2 - hop > place:
                ls[i] = value.astype(jnp.bfloat16)
                l_copy(i).start()
            elif place == 0 or place >= n // 2:
                wg_ref[pl.ds((i % PARTS) * part, part), :] = value.T
            else:
                total[:, columns] = value

    events = []
    for i in range(items):
        for hop in range(n - 1 - i // PARTS):
            due = 6.0 + 26.0 * (i + 1) / items + 2.5 * hop
            events.append((due, functools.partial(add_right, hop=hop), i))
            events.append((due, functools.partial(add_left, hop=hop), i))
    events += [(11.0 + 2.6 * (i + 1), do_odd, k) for i, k in enumerate(ORDER)]
    events += [(11.0 + 3.4 * (i + 1), do_two, k) for i, k in enumerate(NEAR)]
    events += [(10.0 + 3.4 * (i + 1), pass_on, k) for i, k in enumerate(FAR)]
    events += [(30.0 + i, finish, k) for i, k in enumerate(FAR)]
    for _, act, index in sorted(events, key=lambda e: e[0]):
        act(index)

    @pl.when(p < sections - 1)
    def _():
        for k in NEAR:
            y_copy(k).wait_recv()

    @pl.when((p == 0) | (p == 2))
    def _():
        for k in FAR:
            y_copy(k).wait_recv()

    @pl.when(p > 0)
    def _():
        for k in NEAR:
            x_copy(k).wait_send()
            y_copy(k).wait_send()

    @pl.when((p == 1) | (p == 3))
    def _():
        for k in FAR:
            x_copy(k).wait_send()
            y_copy(k).wait_send()

    @pl.when(p == 2)
    def _():
        for k in FAR:
            f_copy(k).wait_send()
            h_copy(k).wait_send()

    @pl.when(p == 1)
    def _():
        for k in FAR:
            o_copy(k).wait_send()

    for i in range(items):

        @pl.when(z < n - 1 - i // PARTS)
        def _():
            r_copy(i).wait_send()

        @pl.when(z > i // PARTS)
        def _():
            l_copy(i).wait_send()


def copy_kernel(in_from, wg_from, in_to, wg_to, in_mid, wg_mid, first, last):
    tokens, rows = in_from.shape[0] // 4, wg_from.shape[0] // 4
    arrive, leave = [], []
    for i in range(4):
        pairs = ((in_from, in_mid, in_to, tokens, i), (wg_from, wg_mid, wg_to, rows, 4 + i))
        for source, middle, target, size, slot in pairs:
            cut = pl.ds(i * size, size)
            arrive.append(pltpu.make_async_copy(source.at[cut], middle.at[cut], first.at[slot]))
            leave.append(pltpu.make_async_copy(middle.at[cut], target.at[cut], last.at[slot]))
    for copy in arrive:
        copy.start()
    for before, after in zip(arrive, leave):
        before.wait()
        after.start()
    for copy in leave:
        copy.wait()


def fused_body(n, sections, grad_out, qkv_saved, w_out, w_qkv, plan):
    _, micro, _, seq, features = grad_out.shape
    head = w_out.shape[-1]
    half = seq // 2
    rows = BMICRO * half
    width = features // PIECES
    part = features // n // PARTS
    items = (n - 1) * PARTS
    low, full = jnp.bfloat16, jnp.float32
    dma = pltpu.SemaphoreType.DMA
    strip = (items, head, part)
    term = (PIECES, rows, width)
    anywhere = pl.BlockSpec(memory_space=pl.ANY)
    vmem = pl.BlockSpec(memory_space=pltpu.VMEM)
    received, weight_grad = pl.pallas_call(
        functools.partial(fused_kernel, (n, sections, micro, seq, head, features)),
        out_shape=(
            jax.ShapeDtypeStruct((half, BMICRO, features), low),
            jax.ShapeDtypeStruct((features // n, head), full),
        ),
        in_specs=[pl.BlockSpec(memory_space=pltpu.SMEM)] + [anywhere] * 4,
        out_specs=(vmem, vmem),
        scratch_shapes=[
            pltpu.VMEM((micro, seq, features), low),
            pltpu.VMEM((micro, seq, 3 * head), low),
            pltpu.VMEM((features, head), low),
            pltpu.VMEM((features, 3 * head), low),
            pltpu.VMEM((micro, seq, seq), full),
            pltpu.VMEM((micro, seq, head), low),
            pltpu.VMEM((head, micro * seq), low),
            pltpu.VMEM((2 * rows, 3 * head), low),
            pltpu.VMEM((head, features), full),
        ]
        + [pltpu.VMEM(term, low)] * 3
        + [pltpu.VMEM((len(FAR), rows, width), low)] * 3
        + [pltpu.VMEM((PIECES, half, BMICRO, width), low)]
        + [pltpu.VMEM(strip, low)] * 4
        + [dma((4,))]
        + [dma((PIECES,))] * 4
        + [dma((len(FAR),))] * 6
        + [dma((items,))] * 4,
        compiler_params=pltpu.CompilerParams(
            collective_id=0, has_side_effects=True, vmem_limit_bytes=56 * 1024 * 1024
        ),
        cost_estimate=pl.CostEstimate(flops=2_000_000_000, bytes_accessed=14_000_000, transcendentals=40_000),
    )(
        plan,
        grad_out.reshape(micro, seq, features),
        qkv_saved.reshape(micro, seq, 3 * head),
        w_out.reshape(features, head),
        w_qkv.reshape(features, 3 * head),
    )
    received, weight_grad = pl.pallas_call(
        copy_kernel,
        out_shape=(
            jax.ShapeDtypeStruct(received.shape, low),
            jax.ShapeDtypeStruct(weight_grad.shape, full),
        ),
        in_specs=[anywhere] * 2,
        out_specs=(anywhere, anywhere),
        scratch_shapes=[
            pltpu.VMEM(received.shape, low),
            pltpu.VMEM(weight_grad.shape, full),
            dma((8,)),
            dma((8,)),
        ],
        compiler_params=pltpu.CompilerParams(vmem_limit_bytes=63 * 1024 * 1024),
    )(received, weight_grad)
    return (received[None, None], weight_grad[None, :, None, :])


def solution(mesh):
    in_specs = (
        P("pipe", None, "dp", None, None),
        P("pipe", None, "dp", None, "tensor", None),
        P("pipe", None, "tensor", None),
        P("pipe", None, "tensor", None),
        P("pipe", None),
    )
    out_specs = (P("pipe", "dp", "tensor", None, None), P("pipe", "dp", "tensor", None))
    chosen = body
    if (mesh.shape["pipe"], mesh.shape["dp"], mesh.shape["tensor"]) == (4, 4, 2):
        chosen = functools.partial(fused_body, mesh.shape["dp"], mesh.shape["pipe"])
    return jax.shard_map(chosen, mesh=mesh, in_specs=in_specs, out_specs=out_specs, check_vma=False)
```

```python
import functools

import jax
import jax.numpy as jnp
from jax import lax
from jax.experimental import pallas as pl
from jax.experimental.pallas import tpu as pltpu
from jax.sharding import PartitionSpec as P

BMICRO = 2
PIECES = 8
FAR = [0, 2, 4, 6]
NEAR = [1, 3, 5, 7]
ORDER = [1, 0, 3, 2, 5, 4, 7, 6]
PARTS = 4
MESH = pl.DeviceIdType.MESH


def shifted(block, axis, distance):
    devices = range(lax.axis_size(axis))
    route = [(i - distance, i) for i in devices if i - distance in devices]
    return lax.ppermute(block, axis, route)


def head_forward(queries, key_rows, values):
    score_scale = queries.shape[-1] ** (-0.5)
    scores = jnp.dot(queries, key_rows.T, preferred_element_type=jnp.float32) * score_scale
    row_ids = lax.broadcasted_iota(jnp.int32, scores.shape, 0)
    col_ids = lax.broadcasted_iota(jnp.int32, scores.shape, 1)
    scores = jnp.where(col_ids <= row_ids, scores, -1e30)
    row_max = jnp.max(scores, axis=1, keepdims=True)
    weights = jnp.exp(scores - row_max)
    softmax = weights / jnp.sum(weights, axis=1, keepdims=True)
    soft_low = softmax.astype(jnp.bfloat16)
    attended = jnp.dot(soft_low, values, preferred_element_type=jnp.float32).astype(jnp.bfloat16)
    return (softmax, soft_low, attended)


def head_backward(queries, key_rows, values, softmax, soft_low, attended, grad_head):
    score_scale = queries.shape[-1] ** (-0.5)
    row_dot = jnp.sum(
        grad_head.astype(jnp.float32) * attended.astype(jnp.float32), axis=1, keepdims=True
    )
    grad_values = jnp.dot(soft_low.T, grad_head, preferred_element_type=jnp.float32)
    grad_probs = jnp.dot(grad_head, values.T, preferred_element_type=jnp.float32)
    grad_scores = (softmax * (grad_probs - row_dot)).astype(jnp.bfloat16)
    grad_query = jnp.dot(grad_scores, key_rows, preferred_element_type=jnp.float32) * score_scale
    grad_keys = jnp.dot(grad_scores.T, queries, preferred_element_type=jnp.float32) * score_scale
    return jnp.concatenate([grad_query, grad_keys, grad_values], axis=1).astype(jnp.bfloat16)


def body(grad_out, qkv_saved, w_out, w_qkv, plan):
    gradients = grad_out[0, :, 0]
    saved_qkv = qkv_saved[0, :, 0, :, 0]
    out_proj = w_out[0, :, 0]
    qkv_proj = w_qkv[0, :, 0]
    head_size = out_proj.shape[1]
    seq_len = gradients.shape[1]
    queries = saved_qkv[:, :, :head_size]
    key_rows = saved_qkv[:, :, head_size : 2 * head_size]
    values = saved_qkv[:, :, 2 * head_size :]
    softmax, soft_low, attended = jax.vmap(head_forward)(queries, key_rows, values)
    current = plan[0, :BMICRO]
    grad_current = jnp.take(gradients, current, axis=0)
    grad_heads = jnp.einsum(
        "msd,dh->msh", grad_current, out_proj, preferred_element_type=jnp.float32
    ).astype(jnp.bfloat16)
    grad_qkv = jax.vmap(head_backward)(
        jnp.take(queries, current, axis=0),
        jnp.take(key_rows, current, axis=0),
        jnp.take(values, current, axis=0),
        jnp.take(softmax, current, axis=0),
        jnp.take(soft_low, current, axis=0),
        jnp.take(attended, current, axis=0),
        grad_heads,
    )
    share_rows = seq_len // lax.axis_size("tensor")
    partials = jnp.einsum("bsk,dk->sbd", grad_qkv, qkv_proj, preferred_element_type=jnp.float32)
    summed = lax.psum(partials.astype(jnp.bfloat16), "tensor").astype(jnp.float32)
    own_rows = lax.dynamic_slice_in_dim(
        summed, lax.axis_index("tensor") * share_rows, share_rows, 0
    )
    received = shifted(own_rows.astype(jnp.bfloat16), "pipe", -1)
    weight_grad = lax.psum_scatter(
        jnp.einsum("msc,msh->ch", gradients, attended, preferred_element_type=jnp.float32),
        "dp",
        scatter_dimension=0,
        tiled=True,
    )
    return (received[None, None], weight_grad[None, :, None, :])


def mm(left, right, left_dim, right_dim):
    return lax.dot_general(
        left, right, (((left_dim,), (right_dim,)), ((), ())), preferred_element_type=jnp.float32
    )


def fused_kernel(
    sizes, plan_ref, g_hbm, qkv_hbm, wo_hbm, wq_hbm, in_ref, wg_ref,
    g, qkv, wo, wq, probs, att, att_t, gqkv, total, xs, own, xr, fr, hr, fo, ys, rs, rr, ls, lr,
    load_sem, x_send, x_recv, y_send, y_recv, f_send, f_recv, h_send, h_recv, o_send, o_recv, r_send, r_recv, l_send, l_recv,
):
    n, sections, micro, seq, head, features = sizes
    p = lax.axis_index("pipe")
    z = lax.axis_index("dp")
    x = lax.axis_index("tensor")
    scale = head ** (-0.5)
    half = seq // 2
    rows = BMICRO * half
    width = features // PIECES
    chunk = features // n
    part = chunk // PARTS
    items = (n - 1) * PARTS

    loads = [
        pltpu.make_async_copy(src, dst, load_sem.at[i])
        for i, (src, dst) in enumerate(((qkv_hbm, qkv), (g_hbm, g), (wo_hbm, wo), (wq_hbm, wq)))
    ]
    loads[0].start()
    loads[1].start()

    barrier = pltpu.get_barrier_semaphore()

    def greet(target):
        pl.semaphore_signal(barrier, inc=1, device_id=target, device_id_type=MESH)

    @pl.when(z > 0)
    def _():
        greet({"dp": z - 1})

    @pl.when(z < n - 1)
    def _():
        greet({"dp": z + 1})

    @pl.when(p > 0)
    def _():
        greet({"tensor": 1 - x})

    @pl.when(p < sections - 1)
    def _():
        greet({"pipe": p + 1})

    def x_copy(k):
        return pltpu.make_async_remote_copy(
            src_ref=xs.at[k], dst_ref=xr.at[k], send_sem=x_send.at[k], recv_sem=x_recv.at[k],
            device_id={"tensor": 1 - x}, device_id_type=MESH,
        )

    def y_copy(k):
        return pltpu.make_async_remote_copy(
            src_ref=ys.at[k], dst_ref=in_ref.at[:, :, pl.ds(k * width, width)],
            send_sem=y_send.at[k], recv_sem=y_recv.at[k],
            device_id={"pipe": p - 1}, device_id_type=MESH,
        )

    def f_copy(k):
        return pltpu.make_async_remote_copy(
            src_ref=xs.at[k], dst_ref=fr.at[k // 2], send_sem=f_send.at[k // 2], recv_sem=f_recv.at[k // 2],
            device_id={"pipe": p - 1}, device_id_type=MESH,
        )

    def h_copy(k):
        return pltpu.make_async_remote_copy(
            src_ref=own.at[k], dst_ref=hr.at[k // 2], send_sem=h_send.at[k // 2], recv_sem=h_recv.at[k // 2],
            device_id={"pipe": p - 1}, device_id_type=MESH,
        )

    def o_copy(k):
        return pltpu.make_async_remote_copy(
            src_ref=fr.at[k // 2], dst_ref=fo.at[k // 2], send_sem=o_send.at[k // 2], recv_sem=o_recv.at[k // 2],
            device_id={"tensor": 1 - x}, device_id_type=MESH,
        )

    def r_copy(i):
        return pltpu.make_async_remote_copy(
            src_ref=rs.at[i], dst_ref=rr.at[i], send_sem=r_send.at[i], recv_sem=r_recv.at[i],
            device_id={"dp": z + 1}, device_id_type=MESH,
        )

    def l_copy(i):
        return pltpu.make_async_remote_copy(
            src_ref=ls.at[i], dst_ref=lr.at[i], send_sem=l_send.at[i], recv_sem=l_recv.at[i],
            device_id={"dp": z - 1}, device_id_type=MESH,
        )

    def r_columns(i):
        return pl.ds((n - 1 - i // PARTS) * chunk + (i % PARTS) * part, part)

    def l_columns(i):
        return pl.ds((i // PARTS) * chunk + (i % PARTS) * part, part)

    loads[0].wait()
    keep = lax.broadcasted_iota(jnp.int32, (seq, seq), 1) <= lax.broadcasted_iota(jnp.int32, (seq, seq), 0)
    softs = []
    for m in range(micro):
        scores = mm(qkv[m, :, :head], qkv[m, :, head : 2 * head], 1, 1) * scale
        scores = jnp.where(keep, scores, -1e30)
        weights = jnp.exp(scores - jnp.max(scores, axis=1, keepdims=True))
        softs.append(weights / jnp.sum(weights, axis=1, keepdims=True))
    outs = [
        mm(softs[m].astype(jnp.bfloat16), qkv[m, :, 2 * head :], 1, 0).astype(jnp.bfloat16)
        for m in range(micro)
    ]
    for m in range(micro):
        probs[m] = softs[m]
        att[m] = outs[m]
    att_t[...] = jnp.concatenate(outs, axis=0).T
    loads[2].start()
    loads[3].start()

    peers = lax.div(z + n - 1, n) + lax.div(2 * n - 2 - z, n) + 2 * lax.div(p + sections - 1, sections)
    pl.semaphore_wait(barrier, peers)

    loads[1].wait()

    upper = lax.div(z, n // 2)

    def product(i):
        place = upper * (i // PARTS) + (1 - upper) * (n - 1 - i // PARTS)
        columns = pl.ds(pl.multiple_of(place * chunk + (i % PARTS) * part, part), part)
        value = mm(
            att_t[...], g[:, :, columns].reshape(micro * seq, part), 1, 0
        )
        total[:, columns] = value
        if i < items:

            @pl.when(z == 0)
            def _():
                rs[i] = value.astype(jnp.bfloat16)
                r_copy(i).start()

            @pl.when(z == n - 1)
            def _():
                ls[i] = value.astype(jnp.bfloat16)
                l_copy(i).start()

    for i in range(PARTS):
        product(i)

    @pl.when(p == 0)
    def _():
        loads[2].wait()
        loads[3].wait()

    @pl.when(p > 0)
    def _():
        loads[2].wait()
        chosen = [plan_ref[0, j] for j in range(BMICRO)]
        acc = jnp.zeros((BMICRO * seq, head), jnp.float32)
        for k in range(PIECES):
            columns = pl.ds(k * width, width)
            lhs = jnp.concatenate([g[m, :, columns] for m in chosen], axis=0)
            acc = acc + mm(lhs, wo[columns, :], 1, 0)
        heads = []
        for j in range(BMICRO):
            m = chosen[j]
            grad_head = acc[j * seq : (j + 1) * seq].astype(jnp.bfloat16)
            softmax = probs[m]
            soft_low = softmax.astype(jnp.bfloat16)
            row_dot = jnp.sum(
                grad_head.astype(jnp.float32) * att[m].astype(jnp.float32), axis=1, keepdims=True
            )
            grad_values = mm(soft_low, grad_head, 0, 0)
            grad_probs = mm(grad_head, qkv[m, :, 2 * head :], 1, 1)
            grad_scores = (softmax * (grad_probs - row_dot)).astype(jnp.bfloat16)
            grad_query = mm(grad_scores, qkv[m, :, head : 2 * head], 1, 0) * scale
            grad_keys = mm(grad_scores, qkv[m, :, :head], 0, 0) * scale
            heads.append(jnp.concatenate([grad_query, grad_keys, grad_values], axis=1).astype(jnp.bfloat16))
        row = lax.broadcasted_iota(jnp.int32, (2 * rows, 2 * rows), 0)
        column = lax.broadcasted_iota(jnp.int32, (2 * rows, 2 * rows), 1)
        second = (row >= rows).astype(jnp.int32)
        side = second * x + (1 - second) * (1 - x)
        inner = row - second * rows
        token = lax.shift_right_logical(inner, 1)
        source = (inner - 2 * token) * seq + side * half + token
        order = (column == source).astype(jnp.bfloat16)
        gqkv[...] = mm(order, jnp.concatenate(heads, axis=0), 1, 0).astype(jnp.bfloat16)
        loads[3].wait()
        for k in ORDER:
            term = mm(gqkv[...], wq[pl.ds(k * width, width), :], 1, 1).astype(jnp.bfloat16)
            xs[k] = term[:rows]
            own[k] = term[rows:]
            if k in FAR:

                @pl.when(p == 2)
                def _():
                    f_copy(k).start()

                @pl.when(p != 2)
                def _():
                    x_copy(k).start()

            else:
                x_copy(k).start()

        @pl.when(p == 2)
        def _():
            for k in FAR:
                h_copy(k).start()

    for i in range(PARTS, items + PARTS):
        product(i)

    @pl.when(p == sections - 1)
    def _():
        in_ref[...] = jnp.zeros_like(in_ref)

    def summed(mine, other):
        value = mine.astype(jnp.float32) + other.astype(jnp.float32)
        return value.reshape(half, BMICRO, width).astype(jnp.bfloat16)

    def do_x(k):
        x_copy(k).wait_recv()
        ys[k] = summed(own[k], xr[k])
        y_copy(k).start()

    def do_odd(k):
        @pl.when((p == 1) | (p == 3))
        def _():
            do_x(k)

    def do_two(k):
        @pl.when(p == 2)
        def _():
            do_x(k)

    def pass_on(k):
        @pl.when(p == 1)
        def _():
            f_copy(k).wait_recv()
            o_copy(k).start()

    def finish(k):
        @pl.when(p == 1)
        def _():
            h_copy(k).wait_recv()
            o_copy(k).wait_recv()
            in_ref[:, :, pl.ds(k * width, width)] = summed(hr[k // 2], fo[k // 2])

    def add_right(i, hop):
        place = n - 1 - i // PARTS
        columns = r_columns(i)

        @pl.when(z == hop + 1)
        def _():
            r_copy(i).wait_recv()
            value = total[:, columns] + rr[i].astype(jnp.float32)
            if hop + 1 < place:
                rs[i] = value.astype(jnp.bfloat16)
                r_copy(i).start()
            elif place == n - 1 or place < n // 2:
                wg_ref[pl.ds((i % PARTS) * part, part), :] = value.T
            else:
                total[:, columns] = value

    def add_left(i, hop):
        place = i // PARTS
        columns = l_columns(i)

        @pl.when(z == n - 2 - hop)
        def _():
            l_copy(i).wait_recv()
            value = total[:, columns] + lr[i].astype(jnp.float32)
            if n - 2 - hop > place:
                ls[i] = value.astype(jnp.bfloat16)
                l_copy(i).start()
            elif place == 0 or place >= n // 2:
                wg_ref[pl.ds((i % PARTS) * part, part), :] = value.T
            else:
                total[:, columns] = value

    events = []
    for i in range(items):
        for hop in range(n - 1 - i // PARTS):
            due = 6.5 + 27.6 * (i + 1) / items + 3.5 * hop
            events.append((due, functools.partial(add_right, hop=hop), i))
            events.append((due, functools.partial(add_left, hop=hop), i))
    events += [(11.0 + 2.6 * (i + 1), do_odd, k) for i, k in enumerate(ORDER)]
    events += [(10.0 + 3.4 * (i + 1), do_two, k) for i, k in enumerate(NEAR)]
    events += [(9.0 + 3.4 * (i + 1), pass_on, k) for i, k in enumerate(FAR)]
    events += [(30.0 + i, finish, k) for i, k in enumerate(FAR)]
    for _, act, index in sorted(events, key=lambda e: e[0]):
        act(index)

    @pl.when(p < sections - 1)
    def _():
        for k in NEAR:
            y_copy(k).wait_recv()

    @pl.when((p == 0) | (p == 2))
    def _():
        for k in FAR:
            y_copy(k).wait_recv()

    @pl.when(p > 0)
    def _():
        for k in NEAR:
            x_copy(k).wait_send()
            y_copy(k).wait_send()

    @pl.when((p == 1) | (p == 3))
    def _():
        for k in FAR:
            x_copy(k).wait_send()
            y_copy(k).wait_send()

    @pl.when(p == 2)
    def _():
        for k in FAR:
            f_copy(k).wait_send()
            h_copy(k).wait_send()

    @pl.when(p == 1)
    def _():
        for k in FAR:
            o_copy(k).wait_send()

    for i in range(items):

        @pl.when(z < n - 1 - i // PARTS)
        def _():
            r_copy(i).wait_send()

        @pl.when(z > i // PARTS)
        def _():
            l_copy(i).wait_send()


def copy_kernel(in_from, wg_from, in_to, wg_to, in_mid, wg_mid, first, last):
    tokens, rows = in_from.shape[0] // 4, wg_from.shape[0] // 4
    arrive, leave = [], []
    for i in range(4):
        pairs = ((in_from, in_mid, in_to, tokens, i), (wg_from, wg_mid, wg_to, rows, 4 + i))
        for source, middle, target, size, slot in pairs:
            cut = pl.ds(i * size, size)
            arrive.append(pltpu.make_async_copy(source.at[cut], middle.at[cut], first.at[slot]))
            leave.append(pltpu.make_async_copy(middle.at[cut], target.at[cut], last.at[slot]))
    for copy in arrive:
        copy.start()
    for before, after in zip(arrive, leave):
        before.wait()
        after.start()
    for copy in leave:
        copy.wait()


def fused_body(n, sections, grad_out, qkv_saved, w_out, w_qkv, plan):
    _, micro, _, seq, features = grad_out.shape
    head = w_out.shape[-1]
    half = seq // 2
    rows = BMICRO * half
    width = features // PIECES
    part = features // n // PARTS
    items = (n - 1) * PARTS
    low, full = jnp.bfloat16, jnp.float32
    dma = pltpu.SemaphoreType.DMA
    strip = (items, head, part)
    term = (PIECES, rows, width)
    anywhere = pl.BlockSpec(memory_space=pl.ANY)
    vmem = pl.BlockSpec(memory_space=pltpu.VMEM)
    received, weight_grad = pl.pallas_call(
        functools.partial(fused_kernel, (n, sections, micro, seq, head, features)),
        out_shape=(
            jax.ShapeDtypeStruct((half, BMICRO, features), low),
            jax.ShapeDtypeStruct((features // n, head), full),
        ),
        in_specs=[pl.BlockSpec(memory_space=pltpu.SMEM)] + [anywhere] * 4,
        out_specs=(vmem, vmem),
        scratch_shapes=[
            pltpu.VMEM((micro, seq, features), low),
            pltpu.VMEM((micro, seq, 3 * head), low),
            pltpu.VMEM((features, head), low),
            pltpu.VMEM((features, 3 * head), low),
            pltpu.VMEM((micro, seq, seq), full),
            pltpu.VMEM((micro, seq, head), low),
            pltpu.VMEM((head, micro * seq), low),
            pltpu.VMEM((2 * rows, 3 * head), low),
            pltpu.VMEM((head, features), full),
        ]
        + [pltpu.VMEM(term, low)] * 3
        + [pltpu.VMEM((len(FAR), rows, width), low)] * 3
        + [pltpu.VMEM((PIECES, half, BMICRO, width), low)]
        + [pltpu.VMEM(strip, low)] * 4
        + [dma((4,))]
        + [dma((PIECES,))] * 4
        + [dma((len(FAR),))] * 6
        + [dma((items,))] * 4,
        compiler_params=pltpu.CompilerParams(
            collective_id=0, has_side_effects=True, vmem_limit_bytes=56 * 1024 * 1024
        ),
        cost_estimate=pl.CostEstimate(flops=2_000_000_000, bytes_accessed=14_000_000, transcendentals=40_000),
    )(
        plan,
        grad_out.reshape(micro, seq, features),
        qkv_saved.reshape(micro, seq, 3 * head),
        w_out.reshape(features, head),
        w_qkv.reshape(features, 3 * head),
    )
    received, weight_grad = pl.pallas_call(
        copy_kernel,
        out_shape=(
            jax.ShapeDtypeStruct(received.shape, low),
            jax.ShapeDtypeStruct(weight_grad.shape, full),
        ),
        in_specs=[anywhere] * 2,
        out_specs=(anywhere, anywhere),
        scratch_shapes=[
            pltpu.VMEM(received.shape, low),
            pltpu.VMEM(weight_grad.shape, full),
            dma((8,)),
            dma((8,)),
        ],
        compiler_params=pltpu.CompilerParams(vmem_limit_bytes=63 * 1024 * 1024),
    )(received, weight_grad)
    return (received[None, None], weight_grad[None, :, None, :])


def solution(mesh):
    in_specs = (
        P("pipe", None, "dp", None, None),
        P("pipe", None, "dp", None, "tensor", None),
        P("pipe", None, "tensor", None),
        P("pipe", None, "tensor", None),
        P("pipe", None),
    )
    out_specs = (P("pipe", "dp", "tensor", None, None), P("pipe", "dp", "tensor", None))
    chosen = body
    if (mesh.shape["pipe"], mesh.shape["dp"], mesh.shape["tensor"]) == (4, 4, 2):
        chosen = functools.partial(fused_body, mesh.shape["dp"], mesh.shape["pipe"])
    return jax.shard_map(chosen, mesh=mesh, in_specs=in_specs, out_specs=out_specs, check_vma=False)
```

```python
import functools

import jax
import jax.numpy as jnp
from jax import lax
from jax.experimental import pallas as pl
from jax.experimental.pallas import tpu as pltpu
from jax.sharding import PartitionSpec as P

BMICRO = 2
PIECES = 8
FAR = [0, 2, 4]
NEAR = [1, 3, 5, 7, 6]
ORDER = [1, 0, 3, 2, 5, 4, 7, 6]
PARTS = 4
MESH = pl.DeviceIdType.MESH


def shifted(block, axis, distance):
    devices = range(lax.axis_size(axis))
    route = [(i - distance, i) for i in devices if i - distance in devices]
    return lax.ppermute(block, axis, route)


def head_forward(queries, key_rows, values):
    score_scale = queries.shape[-1] ** (-0.5)
    scores = jnp.dot(queries, key_rows.T, preferred_element_type=jnp.float32) * score_scale
    row_ids = lax.broadcasted_iota(jnp.int32, scores.shape, 0)
    col_ids = lax.broadcasted_iota(jnp.int32, scores.shape, 1)
    scores = jnp.where(col_ids <= row_ids, scores, -1e30)
    row_max = jnp.max(scores, axis=1, keepdims=True)
    weights = jnp.exp(scores - row_max)
    softmax = weights / jnp.sum(weights, axis=1, keepdims=True)
    soft_low = softmax.astype(jnp.bfloat16)
    attended = jnp.dot(soft_low, values, preferred_element_type=jnp.float32).astype(jnp.bfloat16)
    return (softmax, soft_low, attended)


def head_backward(queries, key_rows, values, softmax, soft_low, attended, grad_head):
    score_scale = queries.shape[-1] ** (-0.5)
    row_dot = jnp.sum(
        grad_head.astype(jnp.float32) * attended.astype(jnp.float32), axis=1, keepdims=True
    )
    grad_values = jnp.dot(soft_low.T, grad_head, preferred_element_type=jnp.float32)
    grad_probs = jnp.dot(grad_head, values.T, preferred_element_type=jnp.float32)
    grad_scores = (softmax * (grad_probs - row_dot)).astype(jnp.bfloat16)
    grad_query = jnp.dot(grad_scores, key_rows, preferred_element_type=jnp.float32) * score_scale
    grad_keys = jnp.dot(grad_scores.T, queries, preferred_element_type=jnp.float32) * score_scale
    return jnp.concatenate([grad_query, grad_keys, grad_values], axis=1).astype(jnp.bfloat16)


def body(grad_out, qkv_saved, w_out, w_qkv, plan):
    gradients = grad_out[0, :, 0]
    saved_qkv = qkv_saved[0, :, 0, :, 0]
    out_proj = w_out[0, :, 0]
    qkv_proj = w_qkv[0, :, 0]
    head_size = out_proj.shape[1]
    seq_len = gradients.shape[1]
    queries = saved_qkv[:, :, :head_size]
    key_rows = saved_qkv[:, :, head_size : 2 * head_size]
    values = saved_qkv[:, :, 2 * head_size :]
    softmax, soft_low, attended = jax.vmap(head_forward)(queries, key_rows, values)
    current = plan[0, :BMICRO]
    grad_current = jnp.take(gradients, current, axis=0)
    grad_heads = jnp.einsum(
        "msd,dh->msh", grad_current, out_proj, preferred_element_type=jnp.float32
    ).astype(jnp.bfloat16)
    grad_qkv = jax.vmap(head_backward)(
        jnp.take(queries, current, axis=0),
        jnp.take(key_rows, current, axis=0),
        jnp.take(values, current, axis=0),
        jnp.take(softmax, current, axis=0),
        jnp.take(soft_low, current, axis=0),
        jnp.take(attended, current, axis=0),
        grad_heads,
    )
    share_rows = seq_len // lax.axis_size("tensor")
    partials = jnp.einsum("bsk,dk->sbd", grad_qkv, qkv_proj, preferred_element_type=jnp.float32)
    summed = lax.psum(partials.astype(jnp.bfloat16), "tensor").astype(jnp.float32)
    own_rows = lax.dynamic_slice_in_dim(
        summed, lax.axis_index("tensor") * share_rows, share_rows, 0
    )
    received = shifted(own_rows.astype(jnp.bfloat16), "pipe", -1)
    weight_grad = lax.psum_scatter(
        jnp.einsum("msc,msh->ch", gradients, attended, preferred_element_type=jnp.float32),
        "dp",
        scatter_dimension=0,
        tiled=True,
    )
    return (received[None, None], weight_grad[None, :, None, :])


def mm(left, right, left_dim, right_dim):
    return lax.dot_general(
        left, right, (((left_dim,), (right_dim,)), ((), ())), preferred_element_type=jnp.float32
    )


def fused_kernel(
    sizes, plan_ref, g_hbm, qkv_hbm, wo_hbm, wq_hbm, in_ref, wg_ref,
    g, qkv, wo, wq, probs, att, att_t, gqkv, total, xs, own, xr, fr, hr, fo, ys, rs, rr, ls, lr,
    load_sem, x_send, x_recv, y_send, y_recv, f_send, f_recv, h_send, h_recv, o_send, o_recv, r_send, r_recv, l_send, l_recv,
):
    n, sections, micro, seq, head, features = sizes
    p = lax.axis_index("pipe")
    z = lax.axis_index("dp")
    x = lax.axis_index("tensor")
    scale = head ** (-0.5)
    half = seq // 2
    rows = BMICRO * half
    width = features // PIECES
    chunk = features // n
    part = chunk // PARTS
    items = (n - 1) * PARTS

    loads = [
        pltpu.make_async_copy(src, dst, load_sem.at[i])
        for i, (src, dst) in enumerate(((qkv_hbm, qkv), (g_hbm, g), (wo_hbm, wo), (wq_hbm, wq)))
    ]
    loads[0].start()
    loads[1].start()

    barrier = pltpu.get_barrier_semaphore()

    def greet(target):
        pl.semaphore_signal(barrier, inc=1, device_id=target, device_id_type=MESH)

    @pl.when(z > 0)
    def _():
        greet({"dp": z - 1})

    @pl.when(z < n - 1)
    def _():
        greet({"dp": z + 1})

    @pl.when(p > 0)
    def _():
        greet({"tensor": 1 - x})

    @pl.when(p < sections - 1)
    def _():
        greet({"pipe": p + 1})

    def x_copy(k):
        return pltpu.make_async_remote_copy(
            src_ref=xs.at[k], dst_ref=xr.at[k], send_sem=x_send.at[k], recv_sem=x_recv.at[k],
            device_id={"tensor": 1 - x}, device_id_type=MESH,
        )

    def y_copy(k):
        return pltpu.make_async_remote_copy(
            src_ref=ys.at[k], dst_ref=in_ref.at[:, :, pl.ds(k * width, width)],
            send_sem=y_send.at[k], recv_sem=y_recv.at[k],
            device_id={"pipe": p - 1}, device_id_type=MESH,
        )

    def f_copy(k):
        return pltpu.make_async_remote_copy(
            src_ref=xs.at[k], dst_ref=fr.at[k // 2], send_sem=f_send.at[k // 2], recv_sem=f_recv.at[k // 2],
            device_id={"pipe": p - 1}, device_id_type=MESH,
        )

    def h_copy(k):
        return pltpu.make_async_remote_copy(
            src_ref=own.at[k], dst_ref=hr.at[k // 2], send_sem=h_send.at[k // 2], recv_sem=h_recv.at[k // 2],
            device_id={"pipe": p - 1}, device_id_type=MESH,
        )

    def o_copy(k):
        return pltpu.make_async_remote_copy(
            src_ref=fr.at[k // 2], dst_ref=fo.at[k // 2], send_sem=o_send.at[k // 2], recv_sem=o_recv.at[k // 2],
            device_id={"tensor": 1 - x}, device_id_type=MESH,
        )

    def r_copy(i):
        return pltpu.make_async_remote_copy(
            src_ref=rs.at[i], dst_ref=rr.at[i], send_sem=r_send.at[i], recv_sem=r_recv.at[i],
            device_id={"dp": z + 1}, device_id_type=MESH,
        )

    def l_copy(i):
        return pltpu.make_async_remote_copy(
            src_ref=ls.at[i], dst_ref=lr.at[i], send_sem=l_send.at[i], recv_sem=l_recv.at[i],
            device_id={"dp": z - 1}, device_id_type=MESH,
        )

    def r_columns(i):
        return pl.ds((n - 1 - i // PARTS) * chunk + (i % PARTS) * part, part)

    def l_columns(i):
        return pl.ds((i // PARTS) * chunk + (i % PARTS) * part, part)

    loads[0].wait()
    keep = lax.broadcasted_iota(jnp.int32, (seq, seq), 1) <= lax.broadcasted_iota(jnp.int32, (seq, seq), 0)
    softs = []
    for m in range(micro):
        scores = mm(qkv[m, :, :head], qkv[m, :, head : 2 * head], 1, 1) * scale
        scores = jnp.where(keep, scores, -1e30)
        weights = jnp.exp(scores - jnp.max(scores, axis=1, keepdims=True))
        softs.append(weights / jnp.sum(weights, axis=1, keepdims=True))
    outs = [
        mm(softs[m].astype(jnp.bfloat16), qkv[m, :, 2 * head :], 1, 0).astype(jnp.bfloat16)
        for m in range(micro)
    ]
    for m in range(micro):
        probs[m] = softs[m]
        att[m] = outs[m]
    att_t[...] = jnp.concatenate(outs, axis=0).T
    loads[2].start()
    loads[3].start()

    peers = lax.div(z + n - 1, n) + lax.div(2 * n - 2 - z, n) + 2 * lax.div(p + sections - 1, sections)
    pl.semaphore_wait(barrier, peers)

    loads[1].wait()

    upper = lax.div(z, n // 2)

    def product(i):
        place = upper * (i // PARTS) + (1 - upper) * (n - 1 - i // PARTS)
        columns = pl.ds(pl.multiple_of(place * chunk + (i % PARTS) * part, part), part)
        value = mm(
            att_t[...], g[:, :, columns].reshape(micro * seq, part), 1, 0
        )
        total[:, columns] = value
        if i < items:

            @pl.when(z == 0)
            def _():
                rs[i] = value.astype(jnp.bfloat16)
                r_copy(i).start()

            @pl.when(z == n - 1)
            def _():
                ls[i] = value.astype(jnp.bfloat16)
                l_copy(i).start()

    for i in range(PARTS):
        product(i)

    @pl.when(p == 0)
    def _():
        loads[2].wait()
        loads[3].wait()

    @pl.when(p > 0)
    def _():
        loads[2].wait()
        chosen = [plan_ref[0, j] for j in range(BMICRO)]
        acc = jnp.zeros((BMICRO * seq, head), jnp.float32)
        for k in range(PIECES):
            columns = pl.ds(k * width, width)
            lhs = jnp.concatenate([g[m, :, columns] for m in chosen], axis=0)
            acc = acc + mm(lhs, wo[columns, :], 1, 0)
        heads = []
        for j in range(BMICRO):
            m = chosen[j]
            grad_head = acc[j * seq : (j + 1) * seq].astype(jnp.bfloat16)
            softmax = probs[m]
            soft_low = softmax.astype(jnp.bfloat16)
            row_dot = jnp.sum(
                grad_head.astype(jnp.float32) * att[m].astype(jnp.float32), axis=1, keepdims=True
            )
            grad_values = mm(soft_low, grad_head, 0, 0)
            grad_probs = mm(grad_head, qkv[m, :, 2 * head :], 1, 1)
            grad_scores = (softmax * (grad_probs - row_dot)).astype(jnp.bfloat16)
            grad_query = mm(grad_scores, qkv[m, :, head : 2 * head], 1, 0) * scale
            grad_keys = mm(grad_scores, qkv[m, :, :head], 0, 0) * scale
            heads.append(jnp.concatenate([grad_query, grad_keys, grad_values], axis=1).astype(jnp.bfloat16))
        row = lax.broadcasted_iota(jnp.int32, (2 * rows, 2 * rows), 0)
        column = lax.broadcasted_iota(jnp.int32, (2 * rows, 2 * rows), 1)
        second = (row >= rows).astype(jnp.int32)
        side = second * x + (1 - second) * (1 - x)
        inner = row - second * rows
        token = lax.shift_right_logical(inner, 1)
        source = (inner - 2 * token) * seq + side * half + token
        order = (column == source).astype(jnp.bfloat16)
        gqkv[...] = mm(order, jnp.concatenate(heads, axis=0), 1, 0).astype(jnp.bfloat16)
        loads[3].wait()
        for k in ORDER:
            term = mm(gqkv[...], wq[pl.ds(k * width, width), :], 1, 1).astype(jnp.bfloat16)
            xs[k] = term[:rows]
            own[k] = term[rows:]
            if k in FAR:

                @pl.when(p == 2)
                def _():
                    f_copy(k).start()

                @pl.when(p != 2)
                def _():
                    x_copy(k).start()

            else:
                x_copy(k).start()

        @pl.when(p == 2)
        def _():
            for k in FAR:
                h_copy(k).start()

    for i in range(PARTS, items + PARTS):
        product(i)

    @pl.when(p == sections - 1)
    def _():
        in_ref[...] = jnp.zeros_like(in_ref)

    def summed(mine, other):
        value = mine.astype(jnp.float32) + other.astype(jnp.float32)
        return value.reshape(half, BMICRO, width).astype(jnp.bfloat16)

    def do_x(k):
        x_copy(k).wait_recv()
        ys[k] = summed(own[k], xr[k])
        y_copy(k).start()

    def do_odd(k):
        @pl.when((p == 1) | (p == 3))
        def _():
            do_x(k)

    def do_two(k):
        @pl.when(p == 2)
        def _():
            do_x(k)

    def pass_on(k):
        @pl.when(p == 1)
        def _():
            f_copy(k).wait_recv()
            o_copy(k).start()

    def finish(k):
        @pl.when(p == 1)
        def _():
            h_copy(k).wait_recv()
            o_copy(k).wait_recv()
            in_ref[:, :, pl.ds(k * width, width)] = summed(hr[k // 2], fo[k // 2])

    def add_right(i, hop):
        place = n - 1 - i // PARTS
        columns = r_columns(i)

        @pl.when(z == hop + 1)
        def _():
            r_copy(i).wait_recv()
            value = total[:, columns] + rr[i].astype(jnp.float32)
            if hop + 1 < place:
                rs[i] = value.astype(jnp.bfloat16)
                r_copy(i).start()
            elif place == n - 1 or place < n // 2:
                wg_ref[pl.ds((i % PARTS) * part, part), :] = value.T
            else:
                total[:, columns] = value

    def add_left(i, hop):
        place = i // PARTS
        columns = l_columns(i)

        @pl.when(z == n - 2 - hop)
        def _():
            l_copy(i).wait_recv()
            value = total[:, columns] + lr[i].astype(jnp.float32)
            if n - 2 - hop > place:
                ls[i] = value.astype(jnp.bfloat16)
                l_copy(i).start()
            elif place == 0 or place >= n // 2:
                wg_ref[pl.ds((i % PARTS) * part, part), :] = value.T
            else:
                total[:, columns] = value

    events = []
    for i in range(items):
        for hop in range(n - 1 - i // PARTS):
            due = 6.5 + 27.6 * (i + 1) / items + 3.5 * hop
            events.append((due, functools.partial(add_right, hop=hop), i))
            events.append((due, functools.partial(add_left, hop=hop), i))
    events += [(11.0 + 2.6 * (i + 1), do_odd, k) for i, k in enumerate(ORDER)]
    events += [(10.0 + 3.4 * (i + 1), do_two, k) for i, k in enumerate(NEAR)]
    events += [(9.0 + 3.4 * (i + 1), pass_on, k) for i, k in enumerate(FAR)]
    events += [(30.0 + i, finish, k) for i, k in enumerate(FAR)]
    for _, act, index in sorted(events, key=lambda e: e[0]):
        act(index)

    @pl.when(p < sections - 1)
    def _():
        for k in NEAR:
            y_copy(k).wait_recv()

    @pl.when((p == 0) | (p == 2))
    def _():
        for k in FAR:
            y_copy(k).wait_recv()

    @pl.when(p > 0)
    def _():
        for k in NEAR:
            x_copy(k).wait_send()
            y_copy(k).wait_send()

    @pl.when((p == 1) | (p == 3))
    def _():
        for k in FAR:
            x_copy(k).wait_send()
            y_copy(k).wait_send()

    @pl.when(p == 2)
    def _():
        for k in FAR:
            f_copy(k).wait_send()
            h_copy(k).wait_send()

    @pl.when(p == 1)
    def _():
        for k in FAR:
            o_copy(k).wait_send()

    for i in range(items):

        @pl.when(z < n - 1 - i // PARTS)
        def _():
            r_copy(i).wait_send()

        @pl.when(z > i // PARTS)
        def _():
            l_copy(i).wait_send()


def copy_kernel(in_from, wg_from, in_to, wg_to, in_mid, wg_mid, first, last):
    tokens, rows = in_from.shape[0] // 4, wg_from.shape[0] // 4
    arrive, leave = [], []
    for i in range(4):
        pairs = ((in_from, in_mid, in_to, tokens, i), (wg_from, wg_mid, wg_to, rows, 4 + i))
        for source, middle, target, size, slot in pairs:
            cut = pl.ds(i * size, size)
            arrive.append(pltpu.make_async_copy(source.at[cut], middle.at[cut], first.at[slot]))
            leave.append(pltpu.make_async_copy(middle.at[cut], target.at[cut], last.at[slot]))
    for copy in arrive:
        copy.start()
    for before, after in zip(arrive, leave):
        before.wait()
        after.start()
    for copy in leave:
        copy.wait()


def fused_body(n, sections, grad_out, qkv_saved, w_out, w_qkv, plan):
    _, micro, _, seq, features = grad_out.shape
    head = w_out.shape[-1]
    half = seq // 2
    rows = BMICRO * half
    width = features // PIECES
    part = features // n // PARTS
    items = (n - 1) * PARTS
    low, full = jnp.bfloat16, jnp.float32
    dma = pltpu.SemaphoreType.DMA
    strip = (items, head, part)
    term = (PIECES, rows, width)
    anywhere = pl.BlockSpec(memory_space=pl.ANY)
    vmem = pl.BlockSpec(memory_space=pltpu.VMEM)
    received, weight_grad = pl.pallas_call(
        functools.partial(fused_kernel, (n, sections, micro, seq, head, features)),
        out_shape=(
            jax.ShapeDtypeStruct((half, BMICRO, features), low),
            jax.ShapeDtypeStruct((features // n, head), full),
        ),
        in_specs=[pl.BlockSpec(memory_space=pltpu.SMEM)] + [anywhere] * 4,
        out_specs=(vmem, vmem),
        scratch_shapes=[
            pltpu.VMEM((micro, seq, features), low),
            pltpu.VMEM((micro, seq, 3 * head), low),
            pltpu.VMEM((features, head), low),
            pltpu.VMEM((features, 3 * head), low),
            pltpu.VMEM((micro, seq, seq), full),
            pltpu.VMEM((micro, seq, head), low),
            pltpu.VMEM((head, micro * seq), low),
            pltpu.VMEM((2 * rows, 3 * head), low),
            pltpu.VMEM((head, features), full),
        ]
        + [pltpu.VMEM(term, low)] * 3
        + [pltpu.VMEM((len(FAR), rows, width), low)] * 3
        + [pltpu.VMEM((PIECES, half, BMICRO, width), low)]
        + [pltpu.VMEM(strip, low)] * 4
        + [dma((4,))]
        + [dma((PIECES,))] * 4
        + [dma((len(FAR),))] * 6
        + [dma((items,))] * 4,
        compiler_params=pltpu.CompilerParams(
            collective_id=0, has_side_effects=True, vmem_limit_bytes=56 * 1024 * 1024
        ),
        cost_estimate=pl.CostEstimate(flops=2_000_000_000, bytes_accessed=14_000_000, transcendentals=40_000),
    )(
        plan,
        grad_out.reshape(micro, seq, features),
        qkv_saved.reshape(micro, seq, 3 * head),
        w_out.reshape(features, head),
        w_qkv.reshape(features, 3 * head),
    )
    received, weight_grad = pl.pallas_call(
        copy_kernel,
        out_shape=(
            jax.ShapeDtypeStruct(received.shape, low),
            jax.ShapeDtypeStruct(weight_grad.shape, full),
        ),
        in_specs=[anywhere] * 2,
        out_specs=(anywhere, anywhere),
        scratch_shapes=[
            pltpu.VMEM(received.shape, low),
            pltpu.VMEM(weight_grad.shape, full),
            dma((8,)),
            dma((8,)),
        ],
        compiler_params=pltpu.CompilerParams(vmem_limit_bytes=63 * 1024 * 1024),
    )(received, weight_grad)
    return (received[None, None], weight_grad[None, :, None, :])


def solution(mesh):
    in_specs = (
        P("pipe", None, "dp", None, None),
        P("pipe", None, "dp", None, "tensor", None),
        P("pipe", None, "tensor", None),
        P("pipe", None, "tensor", None),
        P("pipe", None),
    )
    out_specs = (P("pipe", "dp", "tensor", None, None), P("pipe", "dp", "tensor", None))
    chosen = body
    if (mesh.shape["pipe"], mesh.shape["dp"], mesh.shape["tensor"]) == (4, 4, 2):
        chosen = functools.partial(fused_body, mesh.shape["dp"], mesh.shape["pipe"])
    return jax.shard_map(chosen, mesh=mesh, in_specs=in_specs, out_specs=out_specs, check_vma=False)
```
